128 devices in a mesh: gz: 32 (over x, z, y_lo), gy: 2 (over core), gx: 2 (over y_hi).
Axes of the slice: x: 4, y: 4 (y_hi: 2, y_lo: 2; y = y_hi * 2 + y_lo), z: 4, core: 2. Of those that a mesh axis runs over, the one named last changes fastest.
Arguments:
- positions: float32 [8192, 3, 128], P(('gz', 'gy', 'gx')), may hold values from 0 to 4
- velocities: float32 [8192, 3, 128], P(('gz', 'gy', 'gx')), may hold values from -6 to 6
- charges: float32 [8192, 128], P(('gz', 'gy', 'gx')), may hold values from -4 to 4
- atom_types: int32 [8192, 128], P(('gz', 'gy', 'gx')), may hold values from 0 to 15
- type_radius: float32 [16], replicated, may hold values from 0.3 to 1
- tiles: int32 [32768, 2], P(('gz', 'gy', 'gx')), may hold values from 0 to 383
- tile_live: int32 [128], P(('gz', 'gy', 'gx')), may hold values from 32 to 256, as said below
- destinations: int32 [8192, 1], P(('gz', 'gy', 'gx')), may hold values from 0 to 31; in each aligned block of 64 rows (0 to 63, 64 to 127, ...) at most 4 rows name the same one
Outputs:
- forces: float32 [8192, 3, 128], P(('gz', 'gy', 'gx'))
- arrived: float32 [16384, 8, 128], P(('gz', 'gy', 'gx'))
The draws below stay inside these ranges and needn't reach their ends.
Inputs may be any that keep to these rules, and one draw needn't show every extreme that they name: Each device's used tiles are the first tile_live entries of its list; some device uses all 256. `destinations`: among the rows of one device, at most 4 name the same destination; some destination gets exactly 4 from some device.
All inputs are finite; a program needn't handle non-finite values.
Results may differ from the reference program's by a relative error of at most 0.0003.
Values sent between devices are 32-bit elements; how exact they have to be, the bound alone decides.
A program may use at most 64 MiB of HBM per device.

```python
import math
import jax
import jax.numpy as jnp
import numpy as np
from jax import lax

ATOMS = 128
CL = 64
TILES = 256
NTYPES = 16
STEPS = 2
CAP = 4
NC = 8192
N_GZ = 32
N_GY = 2
N_GX = 2
DEVICES = 128


def draw_tile_live(key, part):
    spread = jax.random.randint(key, (DEVICES,), TILES // 8, TILES + 1)
    busiest = jax.random.randint(jax.random.fold_in(key, 7), (), 0, DEVICES)
    return jnp.where(jnp.arange(DEVICES) == busiest, TILES, spread).astype(jnp.int32)


def place_ends(entries, key, low, top_value):
    spot = [jax.random.randint(jax.random.fold_in(key, axis), (), 0, length) for axis, length in enumerate(entries.shape)]
    widest = entries.shape.index(max(entries.shape))
    next_to = spot[:widest] + [(spot[widest] + 1) % entries.shape[widest]] + spot[widest + 1:]
    return entries.at[tuple(spot)].set(low).at[tuple(next_to)].set(top_value)


def block_scale(key, shape, cuts, low, high):
    def one(dim, shards_of):
        heights = jax.random.uniform(jax.random.fold_in(jax.random.fold_in(key, 6), dim), (shards_of,), jnp.float32, low / len(cuts), high / len(cuts))
        return jnp.repeat(jnp.exp(heights), shape[dim] // shards_of).reshape((-1,) + (1,) * (len(shape) - dim - 1))

    loudness = one(*cuts[0])
    for cut in cuts[1:]:
        loudness = loudness * one(*cut)
    return loudness


def shared_out(own_key, own, number, rows, count, top, limit, slope):
    sequence = jax.random.permutation(own_key, count)
    heavy_load, common = load_shares(count, rows * top, limit, slope, True), load_shares(count, rows * top, limit, slope, False)
    places = jnp.arange(count)

    def named(tallies, offset_by):
        used = int((tallies > 0).sum())
        fixed = max(1, used // 4)
        moved = fixed + (places - fixed + offset_by * (used - fixed)) % max(1, count - fixed)
        return jnp.zeros((count,), jnp.int32).at[sequence[jnp.where(places < fixed, places, moved)]].set(jnp.asarray(tallies, jnp.int32))

    tallies = jnp.where(number % 4 == 0, named(heavy_load, number // 4), named(common, number - number // 4 - 1))
    mixed = jax.random.permutation(jax.random.fold_in(own, 3), count)
    donor, receiver = mixed[0:count // 2 * 2:2], mixed[1:count // 2 * 2:2]
    slack = jnp.minimum(tallies[donor] - 1, limit - tallies[receiver]) // 2
    slack = jnp.where((donor == sequence[0]) | (receiver == sequence[0]) | (tallies[receiver] == 0), 0, jnp.maximum(slack, 0))
    moved = jax.random.randint(jax.random.fold_in(own, 4), (count // 2,), 0, 1 << 20) % (slack + 1)
    tallies = tallies.at[donor].add(-moved).at[receiver].add(moved)
    labels = jnp.searchsorted(jnp.cumsum(tallies), jnp.arange(rows * top), side="right").astype(jnp.int32)
    listing = labels.reshape(top, rows).T
    listing = listing[jax.random.permutation(jax.random.fold_in(own, 1), rows)]
    offset_by = jax.random.randint(jax.random.fold_in(own, 2), (rows, 1), 0, top)
    return jnp.take_along_axis(listing, (jnp.arange(top)[None, :] + offset_by) % top, axis=1)


def load_shares(amount, total, bound, slope, full):
    weights = [(1 << 20) // math.isqrt(standing ** slope) + 1 for standing in range(1, amount + 1)]
    largest = bound if full else min(bound, max(-(-total // amount), total * weights[0] // sum(weights)))
    least = 1 if total - largest >= amount - 1 else 0
    counts, rest = [largest] + [least] * (amount - 1), total - largest - least * (amount - 1)
    while rest > 0:
        free = [i for i in range(1, amount) if counts[i] < largest] or [i for i in range(1, amount) if counts[i] < bound]
        whole, left = sum([weights[i] for i in free]), rest
        for i in free:
            extra = min(bound - counts[i], max(1, left * weights[i] // whole), rest)
            counts[i] = counts[i] + extra
            rest = rest - extra
    return np.array(counts)


def noise(rng, extent, scale, bound, split=(), kind=jnp.bfloat16):
    drawn = scale * jax.random.normal(rng, extent, jnp.float32)
    if split:
        drawn = drawn * block_scale(rng, extent, split, -0.22, 0.18)
    return jnp.clip(drawn, -bound, bound).astype(kind)


def setup_inputs(seed: int = 0) -> dict:
    streams_of = jax.random.split(jax.random.key(seed), 9)
    positions = jnp.clip(4.0 * jax.random.uniform(streams_of[0], (NC, 3, ATOMS), jnp.float32) ** block_scale(streams_of[0], (NC, 3, ATOMS), ((0, 128),), -0.2, 0.2), 0.0, 4.0)
    velocities = noise(streams_of[1], (NC, 3, ATOMS), 1.0, 6.0, ((0, 128),), jnp.float32)
    charges = noise(streams_of[2], (NC, ATOMS), 1.0, 4.0, ((0, 128),), jnp.float32)
    atom_types = place_ends(jax.random.randint(streams_of[3], (NC, ATOMS), 0, NTYPES), jax.random.fold_in(streams_of[3], 1), 0, NTYPES - 1).astype(jnp.int32)
    type_radius = jnp.clip(jnp.exp(jax.random.uniform(streams_of[4], (NTYPES,), jnp.float32, math.log(0.3), math.log(1.0))), 0.3, 1.0)
    tiles = place_ends(jax.random.randint(streams_of[5], (TILES * DEVICES, 2), 0, (N_GY * N_GX + 2) * CL), jax.random.fold_in(streams_of[5], 1), 0, ((N_GY * N_GX + 2) * CL) - 1).astype(jnp.int32)
    tile_live = draw_tile_live(jax.random.fold_in(streams_of[8], 71), 0)
    destinations_keys = jax.random.split(jax.random.fold_in(streams_of[7], 1), NC // CL)
    destinations_turns = jax.random.permutation(jax.random.fold_in(streams_of[7], 3), NC // CL)
    destinations = jax.vmap(lambda own, number: shared_out(jax.random.fold_in(streams_of[7], 2), own, number, CL, N_GZ, 1, CAP, 1))(destinations_keys, destinations_turns).reshape((NC, 1))
    return {"positions": positions, "velocities": velocities, "charges": charges, "atom_types": atom_types, "type_radius": type_radius, "tiles": tiles, "tile_live": tile_live, "destinations": destinations}


coulomb = 0.3
time_step = 0.05
tile_group = 8

def tile_forces(packed, tile_pairs, live_count):
    group_count = tile_pairs.shape[0] // tile_group

    def one_group(group_index, totals):
        first_tile = group_index * tile_group
        chosen = lax.dynamic_slice_in_dim(tile_pairs, first_tile, tile_group, 0)
        left_ids = chosen[:, 0]
        right_ids = chosen[:, 1]
        active = (first_tile + jnp.arange(tile_group, dtype=jnp.int32) < live_count).astype(jnp.float32)
        left_atoms = packed[left_ids]
        right_atoms = packed[right_ids]
        offset = left_atoms[:, 0:3, :, None] - right_atoms[:, 0:3, None, :]
        dist_sq = lax.optimization_barrier(jnp.sum(offset * offset, axis=1))
        soften = left_atoms[:, 4, :, None] + right_atoms[:, 4, None, :]
        denominator = dist_sq + soften * soften
        strength = coulomb * left_atoms[:, 3, :, None] * right_atoms[:, 3, None, :] / (denominator * jnp.sqrt(denominator))
        strength = strength * active[:, None, None]
        pushed = strength[:, None] * offset
        on_left = lax.optimization_barrier(jnp.sum(pushed, axis=3))
        on_right = -lax.optimization_barrier(jnp.sum(pushed, axis=2))
        return totals.at[left_ids].add(on_left).at[right_ids].add(on_right)
    zeros = jnp.zeros((packed.shape[0], 3, packed.shape[2]), jnp.float32)
    return lax.fori_loop(0, group_count, one_group, zeros)

def map_tiles(pieces):
    return tile_forces(pieces[0], pieces[1], pieces[2])

def reference(positions, velocities, charges, atom_types, type_radius, tiles, tile_live, destinations):
    plate_size = N_GY * N_GX
    type_ids = jnp.arange(NTYPES, dtype=jnp.int32)
    atom_radii = lax.optimization_barrier(jnp.sum(jnp.where(atom_types[..., None] == type_ids, type_radius, 0.0), axis=-1))
    tile_pairs = tiles.reshape(DEVICES, TILES, 2)

    def all_forces(places):
        packed = jnp.concatenate([places, charges[:, None], atom_radii[:, None]], axis=1)
        packed = packed.reshape(N_GZ, plate_size, CL, 5, ATOMS)
        plate_rows = jnp.broadcast_to(packed.reshape(N_GZ, 1, plate_size * CL, 5, ATOMS), (N_GZ, plate_size, plate_size * CL, 5, ATOMS))
        lower_block = jnp.roll(packed, 1, axis=0)
        upper_block = jnp.roll(packed, -1, axis=0)
        buffers = jnp.concatenate([plate_rows, lower_block, upper_block], axis=2)
        buffers = buffers.reshape(DEVICES, (plate_size + 2) * CL, 5, ATOMS)
        partial_value = lax.map(map_tiles, (buffers, tile_pairs, tile_live))
        pieces = partial_value.reshape(N_GZ, plate_size, plate_size + 2, CL, 3, ATOMS)
        home_forces = lax.optimization_barrier(jnp.sum(pieces[:, :, :plate_size], axis=1))
        home_forces = home_forces + jnp.roll(pieces[:, :, plate_size], -1, axis=0)
        home_forces = home_forces + jnp.roll(pieces[:, :, plate_size + 1], 1, axis=0)
        return home_forces.reshape(NC, 3, ATOMS)
    places = positions
    moving = velocities
    forces = jnp.zeros_like(positions)
    for step_index in range(STEPS):
        forces = all_forces(places)
        moving = moving + time_step * forces
        places = places + time_step * moving
    carried = jnp.concatenate([places, moving, charges[:, None], atom_radii[:, None]], axis=1)
    carried = carried.reshape(DEVICES, CL, 8, ATOMS)
    target_all = destinations.reshape(DEVICES, CL)
    slot_count = N_GZ * CAP

    def pack_slots(pieces):
        cluster_rows, target_ids = pieces
        onehot = (target_ids[:, None] == jnp.arange(N_GZ, dtype=jnp.int32)[None, :]).astype(jnp.int32)
        rank_before = jnp.cumsum(onehot, axis=0) - onehot
        position = lax.optimization_barrier(jnp.sum(rank_before * onehot, axis=1)) + target_ids * CAP
        select = (position[None, :] == jnp.arange(slot_count, dtype=jnp.int32)[:, None]).astype(jnp.float32)
        return jnp.einsum('sc,cfa->sfa', select, cluster_rows, precision=lax.Precision.HIGHEST)
    sent_slots = lax.map(pack_slots, (carried, target_all))
    sent_slots = sent_slots.reshape(N_GZ, N_GY, N_GX, N_GZ, CAP, 8, ATOMS)
    arrived = jnp.transpose(sent_slots, (3, 1, 2, 0, 4, 5, 6)).reshape(DEVICES * slot_count, 8, ATOMS)
    return (forces, arrived)
```

```python
import functools

import jax
import jax.numpy as jnp
from jax import lax
from jax.experimental import pallas as pl
from jax.experimental.pallas import tpu as pltpu
from jax.sharding import PartitionSpec as P

coulomb = 0.3
time_step = 0.05

MESH = pl.DeviceIdType.MESH
F32 = jnp.float32
BF16 = jnp.bfloat16

CL = 64
LANES = 128
SLOTS = 6
ROWS = SLOTS * CL
CAPACITY = 4
TOWERS = 32
ARRIVING = TOWERS * CAPACITY
UNROLL = 16
CENTER = 2.0
PLANES = 39
ENDS = 20
CHARGED = 31


def split(x):
    high = x.astype(BF16).astype(F32)
    rest = x - high
    middle = rest.astype(BF16).astype(F32)
    return high, middle, rest - middle


def tile_kernel(tiles, live, places, fixed, out, planes, totals):
    def prepare(group, carry):
        slot, inner = group // (CL // 8), group % (CL // 8)
        rows = pl.ds(pl.multiple_of(inner * 8, 8), 8)
        to = pl.multiple_of(group * 8, 8)

        def put(plane, value):
            planes[pl.ds(plane * ROWS + to, 8), :] = value

        x = [places[slot, c, rows, :] - CENTER for c in range(3)]
        q = fixed[slot, 3, rows, :]
        radius = fixed[slot, 4, rows, :]
        half = 0.5 * (x[0] * x[0] + x[1] * x[1] + x[2] * x[2] + radius * radius)
        for c, value in enumerate(x + [radius]):
            high, middle, low = split(value)
            put(c, high)
            put(4 + c, middle)
            put(8 + c, high)
            put(12 + c, low)
            put(16 + c, high)
        parts = split(half)
        one = jnp.ones_like(half)
        for c in range(3):
            put(ENDS + c, one)
            put(ENDS + 3 + c, parts[c])
            put(ENDS + 6 + c, one)
        zero = jnp.zeros_like(half)
        put(ENDS + 9, zero)
        put(ENDS + 10, zero)
        for c, value in enumerate([q * x[0], q * x[1], q * x[2], q]):
            high = value.astype(BF16).astype(F32)
            put(CHARGED + c, high)
            put(CHARGED + 4 + c, value - high)
        for k in range(8):
            totals[pl.ds(pl.multiple_of(group * 64, 64) + k * 8, 8), :] = zero
        return carry

    lax.fori_loop(0, ROWS // 8, prepare, 0)

    sign = jnp.where(lax.broadcasted_iota(jnp.int32, (8, LANES), 0) % 4 == 3, 1.0, -1.0).astype(F32)
    live_count = live[0]

    def eight(plane, row):
        return planes[pl.ds(plane * ROWS + row, 8, stride=ROWS), :]

    def one_group(group, carry):
        sums = []
        ids = [(tiles[0, group * UNROLL + u], tiles[1, group * UNROLL + u]) for u in range(UNROLL)]
        blank = jnp.zeros((32, LANES), F32)
        halves = []
        for u in range(0, UNROLL, 2):
            lefts, rights = [], []
            for a, b in ids[u : u + 2]:
                near = eight(0, a) * sign
                lefts += [near, near, eight(12, a) * sign, eight(ENDS + 3, a)]
                rights.append(jnp.concatenate([eight(0, b), eight(4, b), eight(8, b), eight(ENDS, b)], axis=0))
            left = jnp.concatenate(lefts, axis=0)
            right = jnp.concatenate(
                [
                    jnp.concatenate([rights[0], blank], axis=1),
                    jnp.concatenate([blank, rights[1]], axis=1),
                ],
                axis=0,
            )
            halves.append(
                lax.dot_general(
                    left.astype(BF16), right.astype(BF16), (((0,), (0,)), ((), ())), preferred_element_type=F32
                )
            )
        powers = []
        for half_dist in halves:
            root = lax.rsqrt(half_dist)
            power = root * root * root
            high = power.astype(BF16)
            powers.append((high, (power - high.astype(F32)).astype(BF16)))
        for u in range(0, UNROLL, 2):
            high, low = powers[u // 2]
            active = [
                jnp.where(group * UNROLL + u + v < live_count, 1.0, 0.0).astype(F32) for v in range(2)
            ]
            from_a = jnp.concatenate([eight(CHARGED, ids[u + v][0]) * active[v] for v in range(2)], axis=0).astype(BF16)
            from_b = jnp.concatenate([eight(CHARGED, ids[u + v][1]) * active[v] for v in range(2)], axis=0).astype(BF16)
            on_right = jnp.dot(
                jnp.concatenate([from_a, from_a], axis=1), jnp.concatenate([high, low], axis=0), preferred_element_type=F32
            )
            across = jnp.concatenate(
                [
                    jnp.concatenate([high[:, :LANES], low[:, :LANES]], axis=1),
                    jnp.concatenate([high[:, LANES:], low[:, LANES:]], axis=1),
                ],
                axis=0,
            )
            on_left = lax.dot_general(
                jnp.concatenate([from_b, from_b], axis=1), across, (((1,), (1,)), ((), ())), preferred_element_type=F32
            )
            sums.append((ids[u][0], on_left[0:8, :LANES]))
            sums.append((ids[u][1], on_right[0:8, :LANES]))
            sums.append((ids[u + 1][0], on_left[8:16, LANES:]))
            sums.append((ids[u + 1][1], on_right[8:16, LANES:]))
        for row, value in sums:
            at = pl.ds(pl.multiple_of(row * 8, 8), 8)
            totals[at, :] = totals[at, :] + value
        return carry

    lax.fori_loop(0, (live_count + UNROLL - 1) // UNROLL, one_group, 0)

    factor = coulomb * 0.5**1.5

    def finish(group, carry):
        slot, inner = group // (CL // 8), group % (CL // 8)
        rows = pl.ds(pl.multiple_of(inner * 8, 8), 8)

        def summed(channel):
            first = pl.multiple_of(group * 64, 64) + channel
            return totals[pl.ds(first, 8, stride=8), :] + totals[pl.ds(first + 4, 8, stride=8), :]

        scale = factor * fixed[slot, 3, rows, :]
        whole = summed(3)
        for c in range(3):
            out[slot, c, rows, :] = scale * ((places[slot, c, rows, :] - CENTER) * whole - summed(c))
        return carry

    lax.fori_loop(0, ROWS // 8, finish, 0)


def tile_forces(tiles, live, places, fixed):
    return pl.pallas_call(
        tile_kernel,
        out_shape=jax.ShapeDtypeStruct((SLOTS, 3, CL, LANES), F32),
        in_specs=[
            pl.BlockSpec(memory_space=pltpu.SMEM),
            pl.BlockSpec(memory_space=pltpu.SMEM),
            pl.BlockSpec(memory_space=pltpu.VMEM),
            pl.BlockSpec(memory_space=pltpu.VMEM),
        ],
        out_specs=pl.BlockSpec(memory_space=pltpu.VMEM),
        scratch_shapes=[
            pltpu.VMEM((PLANES * ROWS, LANES), F32),
            pltpu.VMEM((ROWS * 8, LANES), F32),
        ],
        compiler_params=pltpu.CompilerParams(vmem_limit_bytes=40 * 2**20),
        cost_estimate=pl.CostEstimate(flops=256 * 128 * 128 * 120, bytes_accessed=2 * 2**20, transcendentals=256 * 128 * 128),
    )(tiles, live, places, fixed)


VMEM = pl.BlockSpec(memory_space=pltpu.VMEM)
SMEM = pl.BlockSpec(memory_space=pltpu.SMEM)
BELOW, ABOVE = 4, 5


def here():
    return lax.axis_index("gz"), lax.axis_index("gy"), lax.axis_index("gx")


def neighbours():
    z, y, x = here()
    mine = y * 2 + x
    partners = []
    for dy, dx in ((0, 1), (1, 1), (1, 0)):
        oy, ox = (1 - y if dy else y), (1 - x if dx else x)
        partners.append(((z, oy, ox), oy * 2 + ox, mine))
    partners.append(((lax.rem(z + 1, TOWERS), y, x), ABOVE, BELOW))
    partners.append(((lax.rem(z + TOWERS - 1, TOWERS), y, x), BELOW, ABOVE))
    return mine, partners


def greet(devices):
    barrier = pltpu.get_barrier_semaphore()
    for device in devices:
        pl.semaphore_signal(barrier, inc=1, device_id=device, device_id_type=MESH)
    return barrier


def spread(buffer, send_sems, recv_sems):
    mine, partners = neighbours()
    copies = []
    for k, (device, there, back) in enumerate(partners):
        copy = pltpu.make_async_remote_copy(
            buffer.at[mine], buffer.at[back], send_sems.at[k], recv_sems.at[back], device_id=device, device_id_type=MESH
        )
        copy.start()
        copies.append(copy)
    for k, (device, there, back) in enumerate(partners):
        pltpu.make_async_remote_copy(
            buffer.at[there], buffer.at[there], send_sems.at[k], recv_sems.at[there], device_id=device, device_id_type=MESH
        ).wait_recv()
    for copy in copies:
        copy.wait_send()


def gather_forces(partial, landing, send_sems, recv_sems):
    mine, partners = neighbours()
    copies = []
    for k, (device, there, back) in enumerate(partners):
        copy = pltpu.make_async_remote_copy(
            partial.at[there], landing.at[back], send_sems.at[k], recv_sems.at[back], device_id=device, device_id_type=MESH
        )
        copy.start()
        copies.append(copy)
    total = [partial[mine, c] for c in range(3)]
    for k, (device, there, back) in enumerate(partners):
        pltpu.make_async_remote_copy(
            landing.at[there], landing.at[there], send_sems.at[k], recv_sems.at[there], device_id=device, device_id_type=MESH
        ).wait_recv()
        total = [total[c] + landing[there, c] for c in range(3)]
    for copy in copies:
        copy.wait_send()
    return total


def import_kernel(radii, positions, charges, types, buffer, send_sems, recv_sems):
    mine, partners = neighbours()
    barrier = greet([p[0] for p in partners])
    for c in range(3):
        buffer[mine, c] = positions[c]
    buffer[mine, 3] = charges[...]
    kinds = types[...]
    radius = jnp.zeros((CL, LANES), F32)
    for kind in range(16):
        radius = jnp.where(kinds == kind, radii[kind], radius)
    buffer[mine, 4] = radius
    pl.semaphore_wait(barrier, 5)
    spread(buffer, send_sems, recv_sems)


def step_kernel(partial, fixed, velocities, places, moving, landing, send_sems, recv_sems, next_send, next_recv):
    mine, partners = neighbours()
    barrier = greet([p[0] for p in partners])
    pl.semaphore_wait(barrier, 5)
    forces = gather_forces(partial, landing, send_sems, recv_sems)
    for c in range(3):
        speed = velocities[c] + time_step * forces[c]
        moving[c] = speed
        places[mine, c] = fixed[mine, c] + time_step * speed
    spread(places, next_send, next_recv)


def last_kernel(
    partial, fixed, places, moving, destinations, forces_out, arrived, landing, slots, send_sems, recv_sems, out_sems, in_sems, own_sem
):
    z, y, x = here()
    mine, partners = neighbours()
    others = [(lax.rem(z + k, TOWERS), y, x) for k in range(1, TOWERS)]
    barrier = greet([p[0] for p in partners[:3]] + others)

    row = jnp.broadcast_to(destinations[...].astype(F32), (CL, CL))
    r = lax.broadcasted_iota(jnp.int32, (CL, CL), 0)
    c = lax.broadcasted_iota(jnp.int32, (CL, CL), 1)
    column = jnp.sum(jnp.where(r == c, row, 0.0), axis=1, keepdims=True)
    rank = jnp.sum(jnp.where((column == row) & (r < c), 1.0, 0.0), axis=0, keepdims=True)
    slot = row[0:1] * CAPACITY + rank
    select = (lax.broadcasted_iota(jnp.int32, (ARRIVING, CL), 0).astype(F32) == slot).astype(BF16)

    pl.semaphore_wait(barrier, 3 + TOWERS - 1)
    forces = gather_forces(partial, landing, send_sems, recv_sems)
    carried = []
    speeds = []
    for k in range(3):
        forces_out[k] = forces[k]
        speed = moving[k] + time_step * forces[k]
        speeds.append(speed)
        carried.append(places[mine, k] + time_step * speed)
    carried = carried + speeds + [fixed[mine, 3], fixed[mine, 4]]
    for k, value in enumerate(carried):
        parts = split(value)
        slots[:, k, :] = sum(jnp.dot(select, part.astype(BF16), preferred_element_type=F32) for part in reversed(parts))

    def send(tower):
        return pltpu.make_async_remote_copy(
            slots.at[pl.ds(tower * CAPACITY, CAPACITY)],
            arrived.at[pl.ds(z * CAPACITY, CAPACITY)],
            out_sems.at[tower],
            in_sems.at[z],
            device_id=(tower, y, x),
            device_id_type=MESH,
        )

    def receive(tower):
        return pltpu.make_async_remote_copy(
            slots.at[pl.ds(tower * CAPACITY, CAPACITY)],
            arrived.at[pl.ds(tower * CAPACITY, CAPACITY)],
            out_sems.at[tower],
            in_sems.at[tower],
            device_id=(tower, y, x),
            device_id_type=MESH,
        )

    for k in range(1, TOWERS):
        send(lax.rem(z + k, TOWERS)).start()
    own = pltpu.make_async_copy(
        slots.at[pl.ds(z * CAPACITY, CAPACITY)], arrived.at[pl.ds(z * CAPACITY, CAPACITY)], own_sem
    )
    own.start()
    own.wait()
    for k in range(1, TOWERS):
        receive(lax.rem(z + TOWERS - k, TOWERS)).wait_recv()
    for k in range(1, TOWERS):
        send(lax.rem(z + k, TOWERS)).wait_send()


def params(number):
    return pltpu.CompilerParams(collective_id=number, has_side_effects=True, vmem_limit_bytes=40 * 2**20)


def dma(count):
    return pltpu.SemaphoreType.DMA((count,))


def local(positions, velocities, charges, atom_types, type_radius, tiles, tile_live, destinations):
    shape = functools.partial(jax.ShapeDtypeStruct, dtype=F32)
    pairs = tiles.T
    landing = pltpu.VMEM((SLOTS, 3, CL, LANES), F32)
    fixed = pl.pallas_call(
        import_kernel,
        out_shape=shape((SLOTS, 5, CL, LANES)),
        in_specs=[SMEM, VMEM, VMEM, VMEM],
        out_specs=VMEM,
        scratch_shapes=[dma(5), dma(6)],
        compiler_params=params(0),
    )(type_radius, jnp.swapaxes(positions, 0, 1), charges, atom_types)
    partial = tile_forces(pairs, tile_live, fixed, fixed)
    places, moving = pl.pallas_call(
        step_kernel,
        out_shape=(shape((SLOTS, 3, CL, LANES)), shape((3, CL, LANES))),
        in_specs=[VMEM] * 3,
        out_specs=(VMEM, VMEM),
        scratch_shapes=[landing, dma(5), dma(6), dma(5), dma(6)],
        compiler_params=params(1),
    )(partial, fixed, jnp.swapaxes(velocities, 0, 1))
    partial = tile_forces(pairs, tile_live, places, fixed)
    forces, arrived = pl.pallas_call(
        last_kernel,
        out_shape=(shape((3, CL, LANES)), shape((ARRIVING, 8, LANES))),
        in_specs=[VMEM] * 5,
        out_specs=(VMEM, VMEM),
        scratch_shapes=[
            landing,
            pltpu.VMEM((ARRIVING, 8, LANES), F32),
            dma(5),
            dma(6),
            dma(TOWERS),
            dma(TOWERS),
            pltpu.SemaphoreType.DMA,
        ],
        compiler_params=params(2),
    )(partial, fixed, places, moving, destinations.T)
    return jnp.swapaxes(forces, 0, 1), arrived


def solution(mesh):
    home = ("gz", "gy", "gx")
    placed = (
        P(home, None, None),
        P(home, None, None),
        P(home, None),
        P(home, None),
        P(),
        P(home, None),
        P(home),
        P(home, None),
    )
    return jax.shard_map(
        local,
        mesh=mesh,
        in_specs=placed,
        out_specs=(P(home, None, None), P(home, None, None)),
        check_vma=False,
    )
```

```python
import functools

import jax
import jax.numpy as jnp
from jax import lax
from jax.experimental import pallas as pl
from jax.experimental.pallas import tpu as pltpu
from jax.sharding import PartitionSpec as P

coulomb = 0.3
time_step = 0.05

MESH = pl.DeviceIdType.MESH
F32 = jnp.float32
BF16 = jnp.bfloat16

CL = 64
LANES = 128
SLOTS = 6
ROWS = SLOTS * CL
CAPACITY = 4
TOWERS = 32
ARRIVING = TOWERS * CAPACITY
UNROLL = 16
CENTER = 2.0
PLANES = 39
ENDS = 20
CHARGED = 31


def split(x):
    high = x.astype(BF16).astype(F32)
    rest = x - high
    middle = rest.astype(BF16).astype(F32)
    return high, middle, rest - middle


def tile_kernel(tiles, live, places, fixed, out, planes, totals):
    def prepare(group, carry):
        slot, inner = group // (CL // 8), group % (CL // 8)
        rows = pl.ds(pl.multiple_of(inner * 8, 8), 8)
        to = pl.multiple_of(group * 8, 8)

        def put(plane, value):
            planes[pl.ds(plane * ROWS + to, 8), :] = value

        x = [places[slot, c, rows, :] - CENTER for c in range(3)]
        q = fixed[slot, 3, rows, :]
        radius = fixed[slot, 4, rows, :]
        half = 0.5 * (x[0] * x[0] + x[1] * x[1] + x[2] * x[2] + radius * radius)
        for c, value in enumerate(x + [radius]):
            high, middle, low = split(value)
            put(c, high)
            put(4 + c, middle)
            put(8 + c, high)
            put(12 + c, low)
            put(16 + c, high)
        parts = split(half)
        one = jnp.ones_like(half)
        for c in range(3):
            put(ENDS + c, one)
            put(ENDS + 3 + c, parts[c])
            put(ENDS + 6 + c, one)
        zero = jnp.zeros_like(half)
        put(ENDS + 9, zero)
        put(ENDS + 10, zero)
        for c, value in enumerate([q * x[0], q * x[1], q * x[2], q]):
            high = value.astype(BF16).astype(F32)
            put(CHARGED + c, high)
            put(CHARGED + 4 + c, value - high)
        for k in range(8):
            totals[pl.ds(pl.multiple_of(group * 64, 64) + k * 8, 8), :] = zero
        return carry

    lax.fori_loop(0, ROWS // 8, prepare, 0)

    sign = jnp.where(lax.broadcasted_iota(jnp.int32, (8, LANES), 0) % 4 == 3, 1.0, -1.0).astype(F32)
    live_count = live[0]

    def eight(plane, row):
        return planes[pl.ds(plane * ROWS + row, 8, stride=ROWS), :]

    def one_group(group, carry):
        sums = []
        ids = [(tiles[0, group * UNROLL + u], tiles[1, group * UNROLL + u]) for u in range(UNROLL)]
        blank = jnp.zeros((32, LANES), F32)
        halves = []
        for u in range(0, UNROLL, 2):
            lefts, rights = [], []
            for a, b in ids[u : u + 2]:
                near = eight(0, a) * sign
                lefts += [near, near, eight(12, a) * sign, eight(ENDS + 3, a)]
                rights.append(jnp.concatenate([eight(0, b), eight(4, b), eight(8, b), eight(ENDS, b)], axis=0))
            left = jnp.concatenate(lefts, axis=0)
            right = jnp.concatenate(
                [
                    jnp.concatenate([rights[0], blank], axis=1),
                    jnp.concatenate([blank, rights[1]], axis=1),
                ],
                axis=0,
            )
            halves.append(
                lax.dot_general(
                    left.astype(BF16), right.astype(BF16), (((0,), (0,)), ((), ())), preferred_element_type=F32
                )
            )
        powers = []
        for half_dist in halves:
            root = lax.rsqrt(half_dist)
            power = root * root * root
            high = power.astype(BF16)
            powers.append((high, (power - high.astype(F32)).astype(BF16)))
        for u in range(0, UNROLL, 2):
            high, low = powers[u // 2]
            active = [
                jnp.where(group * UNROLL + u + v < live_count, 1.0, 0.0).astype(F32) for v in range(2)
            ]
            from_a = jnp.concatenate([eight(CHARGED, ids[u + v][0]) * active[v] for v in range(2)], axis=0).astype(BF16)
            from_b = jnp.concatenate([eight(CHARGED, ids[u + v][1]) * active[v] for v in range(2)], axis=0).astype(BF16)
            on_right = jnp.dot(
                jnp.concatenate([from_a, from_a], axis=1), jnp.concatenate([high, low], axis=0), preferred_element_type=F32
            )
            across = jnp.concatenate(
                [
                    jnp.concatenate([high[:, :LANES], low[:, :LANES]], axis=1),
                    jnp.concatenate([high[:, LANES:], low[:, LANES:]], axis=1),
                ],
                axis=0,
            )
            on_left = lax.dot_general(
                jnp.concatenate([from_b, from_b], axis=1), across, (((1,), (1,)), ((), ())), preferred_element_type=F32
            )
            sums.append((ids[u][0], on_left[0:8, :LANES]))
            sums.append((ids[u][1], on_right[0:8, :LANES]))
            sums.append((ids[u + 1][0], on_left[8:16, LANES:]))
            sums.append((ids[u + 1][1], on_right[8:16, LANES:]))
        for row, value in sums:
            at = pl.ds(pl.multiple_of(row * 8, 8), 8)
            totals[at, :] = totals[at, :] + value
        return carry

    lax.fori_loop(0, (live_count + UNROLL - 1) // UNROLL, one_group, 0)

    factor = coulomb * 0.5**1.5

    def finish(group, carry):
        slot, inner = group // (CL // 8), group % (CL // 8)
        rows = pl.ds(pl.multiple_of(inner * 8, 8), 8)

        def summed(channel):
            first = pl.multiple_of(group * 64, 64) + channel
            return totals[pl.ds(first, 8, stride=8), :] + totals[pl.ds(first + 4, 8, stride=8), :]

        scale = factor * fixed[slot, 3, rows, :]
        whole = summed(3)
        for c in range(3):
            out[slot, c, rows, :] = scale * ((places[slot, c, rows, :] - CENTER) * whole - summed(c))
        return carry

    lax.fori_loop(0, ROWS // 8, finish, 0)


def tile_forces(tiles, live, places, fixed):
    return pl.pallas_call(
        tile_kernel,
        out_shape=jax.ShapeDtypeStruct((SLOTS, 3, CL, LANES), F32),
        in_specs=[
            pl.BlockSpec(memory_space=pltpu.SMEM),
            pl.BlockSpec(memory_space=pltpu.SMEM),
            pl.BlockSpec(memory_space=pltpu.VMEM),
            pl.BlockSpec(memory_space=pltpu.VMEM),
        ],
        out_specs=pl.BlockSpec(memory_space=pltpu.VMEM),
        scratch_shapes=[
            pltpu.VMEM((PLANES * ROWS, LANES), F32),
            pltpu.VMEM((ROWS * 8, LANES), F32),
        ],
        compiler_params=pltpu.CompilerParams(vmem_limit_bytes=40 * 2**20),
        cost_estimate=pl.CostEstimate(flops=256 * 128 * 128 * 120, bytes_accessed=2 * 2**20, transcendentals=256 * 128 * 128),
    )(tiles, live, places, fixed)


VMEM = pl.BlockSpec(memory_space=pltpu.VMEM)
HBM = pl.BlockSpec(memory_space=pltpu.HBM)
SMEM = pl.BlockSpec(memory_space=pltpu.SMEM)
BELOW, ABOVE = 4, 5


def here():
    return lax.axis_index("gz"), lax.axis_index("gy"), lax.axis_index("gx")


def neighbours():
    z, y, x = here()
    even = lax.rem(z, 2) == 0
    step = 1 - 2 * lax.rem(z, 2)
    pair = z + step
    return dict(
        core=(z, 1 - y, x),
        pair=(pair, y, x),
        cross=(pair, y, 1 - x),
        ahead=(lax.rem(z + 2 * step + TOWERS, TOWERS), y, x),
        behind=(lax.rem(z - 2 * step + TOWERS, TOWERS), y, x),
        mine=y * 2 + x,
        core_slot=(1 - y) * 2 + x,
        plate_slot=y * 2 + 1 - x,
        far_slot=(1 - y) * 2 + 1 - x,
        pair_slot=ABOVE - lax.rem(z, 2),
        other_slot=BELOW + lax.rem(z, 2),
    )


PARTNERS = ("core", "pair", "cross", "ahead", "behind")


def greet(devices):
    barrier = pltpu.get_barrier_semaphore()
    for device in devices:
        pl.semaphore_signal(barrier, inc=1, device_id=device, device_id_type=MESH)
    return barrier


def remote(source, target, send_sems, recv_sems, way, chunk, device):
    return pltpu.make_async_remote_copy(
        source, target, send_sems.at[way, chunk], recv_sems.at[way, chunk], device_id=device, device_id_type=MESH
    )


def spread(n, buffer, count, send_sems, recv_sems, ready=None):
    sent = []

    def send(way, chunk, slot, there, name):
        copy = remote(buffer.at[slot, chunk], buffer.at[there, chunk], send_sems, recv_sems, way, chunk, n[name])
        copy.start()
        sent.append(copy)

    def arrive(way, chunk, slot):
        remote(buffer.at[slot, chunk], buffer.at[slot, chunk], send_sems, recv_sems, way, chunk, n["core"]).wait_recv()

    for c in range(count):
        if ready:
            ready(c)
        send(1, c, n["mine"], n["other_slot"], "pair")
        send(0, c, n["mine"], n["mine"], "core")
    for c in range(count):
        arrive(1, c, n["pair_slot"])
        send(2, c, n["pair_slot"], n["mine"], "cross")
        send(3, c, n["pair_slot"], n["other_slot"], "ahead")
    for c in range(count):
        arrive(2, c, n["plate_slot"])
        send(4, c, n["plate_slot"], n["plate_slot"], "core")
    for c in range(count):
        arrive(0, c, n["core_slot"])
        arrive(3, c, n["other_slot"])
        arrive(4, c, n["far_slot"])
    for copy in sent:
        copy.wait_send()


def gather_forces(n, partial, landing, send_sems, recv_sems):
    sent = []

    def send(way, chunk, source, name):
        copy = remote(source, landing.at[way, chunk], send_sems, recv_sems, way, chunk, n[name])
        copy.start()
        sent.append(copy)

    def arrive(way, chunk):
        place = landing.at[way, chunk]
        remote(place, place, send_sems, recv_sems, way, chunk, n["core"]).wait_recv()

    for c in range(3):
        send(0, c, partial.at[n["far_slot"], c], "core")
        send(2, c, partial.at[n["other_slot"], c], "behind")
    for c in range(3):
        send(4, c, partial.at[n["core_slot"], c], "core")
    for c in range(3):
        arrive(0, c)
        landing[5, c] = partial[n["plate_slot"], c] + landing[0, c]
        send(1, c, landing.at[5, c], "cross")
    for c in range(3):
        arrive(1, c)
        arrive(2, c)
        landing[6, c] = partial[n["pair_slot"], c] + landing[1, c] + landing[2, c]
        send(3, c, landing.at[6, c], "pair")
    total = []
    for c in range(3):
        arrive(3, c)
        arrive(4, c)
        total.append(partial[n["mine"], c] + landing[3, c] + landing[4, c])
    return total, sent


def import_kernel(radii, positions, charges, types, buffer, kinds, table, load_sems, send_sems, recv_sems):
    n = neighbours()
    mine = n["mine"]
    loads = [pltpu.make_async_copy(positions.at[c], buffer.at[mine, c], load_sems.at[c]) for c in range(3)]
    loads.append(pltpu.make_async_copy(charges, buffer.at[mine, 3], load_sems.at[3]))
    loads.append(pltpu.make_async_copy(types, kinds, load_sems.at[4]))
    loads.append(pltpu.make_async_copy(radii, table, load_sems.at[5]))
    for load in loads:
        load.start()
    barrier = greet([n[name] for name in PARTNERS])
    pl.semaphore_wait(barrier, len(PARTNERS))

    def ready(c):
        loads[c].wait()
        if c == 4:
            loads[5].wait()
            radius = jnp.zeros((CL, LANES), F32)
            for kind in range(16):
                radius = jnp.where(kinds[...] == kind, table[kind], radius)
            buffer[mine, 4] = radius

    spread(n, buffer, 5, send_sems, recv_sems, ready)


def step_kernel(partial, fixed, velocities, places, moving, landing, send_sems, recv_sems, next_send, next_recv):
    n = neighbours()
    mine = n["mine"]
    barrier = greet([n[name] for name in PARTNERS])
    pl.semaphore_wait(barrier, len(PARTNERS))
    forces, sent = gather_forces(n, partial, landing, send_sems, recv_sems)
    for c in range(3):
        speed = velocities[c] + time_step * forces[c]
        moving[c] = speed
        places[mine, c] = fixed[mine, c] + time_step * speed
    spread(n, places, 3, next_send, next_recv)
    for copy in sent:
        copy.wait_send()


def last_kernel(
    partial, fixed, places, moving, destinations, forces_out, arrived, landing, slots, send_sems, recv_sems, out_sems, in_sems, own_sem
):
    z, y, x = here()
    n = neighbours()
    mine = n["mine"]
    others = [(lax.rem(z + k, TOWERS), y, x) for k in range(1, TOWERS)]
    barrier = greet([n["core"], n["cross"]] + others)

    row = jnp.broadcast_to(destinations[...].astype(F32), (CL, CL))
    r = lax.broadcasted_iota(jnp.int32, (CL, CL), 0)
    c = lax.broadcasted_iota(jnp.int32, (CL, CL), 1)
    column = jnp.sum(jnp.where(r == c, row, 0.0), axis=1, keepdims=True)
    rank = jnp.sum(jnp.where((column == row) & (r < c), 1.0, 0.0), axis=0, keepdims=True)
    slot = row[0:1] * CAPACITY + rank
    select = (lax.broadcasted_iota(jnp.int32, (ARRIVING, CL), 0).astype(F32) == slot).astype(BF16)

    pl.semaphore_wait(barrier, 2 + TOWERS - 1)
    forces, sent = gather_forces(n, partial, landing, send_sems, recv_sems)
    carried = []
    speeds = []
    for k in range(3):
        forces_out[k] = forces[k]
        speed = moving[k] + time_step * forces[k]
        speeds.append(speed)
        carried.append(places[mine, k] + time_step * speed)
    carried = carried + speeds + [fixed[mine, 3], fixed[mine, 4]]
    for k, value in enumerate(carried):
        parts = split(value)
        slots[:, k, :] = sum(jnp.dot(select, part.astype(BF16), preferred_element_type=F32) for part in reversed(parts))

    def send(tower):
        return pltpu.make_async_remote_copy(
            slots.at[pl.ds(tower * CAPACITY, CAPACITY)],
            arrived.at[pl.ds(z * CAPACITY, CAPACITY)],
            out_sems.at[tower],
            in_sems.at[z],
            device_id=(tower, y, x),
            device_id_type=MESH,
        )

    def receive(tower):
        return pltpu.make_async_remote_copy(
            slots.at[pl.ds(tower * CAPACITY, CAPACITY)],
            arrived.at[pl.ds(tower * CAPACITY, CAPACITY)],
            out_sems.at[tower],
            in_sems.at[tower],
            device_id=(tower, y, x),
            device_id_type=MESH,
        )

    for k in range(1, TOWERS):
        send(lax.rem(z + k, TOWERS)).start()
    own = pltpu.make_async_copy(
        slots.at[pl.ds(z * CAPACITY, CAPACITY)], arrived.at[pl.ds(z * CAPACITY, CAPACITY)], own_sem
    )
    own.start()
    own.wait()
    for k in range(1, TOWERS):
        receive(lax.rem(z + TOWERS - k, TOWERS)).wait_recv()
    for k in range(1, TOWERS):
        send(lax.rem(z + k, TOWERS)).wait_send()
    for copy in sent:
        copy.wait_send()


def params(number):
    return pltpu.CompilerParams(collective_id=number, has_side_effects=True, vmem_limit_bytes=40 * 2**20)


def dma(*counts):
    return pltpu.SemaphoreType.DMA(counts)


def local(positions, velocities, charges, atom_types, type_radius, tiles, tile_live, destinations):
    shape = functools.partial(jax.ShapeDtypeStruct, dtype=F32)
    pairs = tiles.T
    landing = pltpu.VMEM((7, 3, CL, LANES), F32)
    fixed = pl.pallas_call(
        import_kernel,
        out_shape=shape((SLOTS, 5, CL, LANES)),
        in_specs=[HBM] * 4,
        out_specs=VMEM,
        scratch_shapes=[pltpu.VMEM((CL, LANES), jnp.int32), pltpu.SMEM((16,), F32), dma(6), dma(5, 5), dma(5, 5)],
        compiler_params=params(0),
    )(type_radius, jnp.swapaxes(positions, 0, 1), charges, atom_types)
    partial = tile_forces(pairs, tile_live, fixed, fixed)
    places, moving = pl.pallas_call(
        step_kernel,
        out_shape=(shape((SLOTS, 3, CL, LANES)), shape((3, CL, LANES))),
        in_specs=[VMEM] * 3,
        out_specs=(VMEM, VMEM),
        scratch_shapes=[landing, dma(5, 3), dma(5, 3), dma(5, 3), dma(5, 3)],
        compiler_params=params(1),
    )(partial, fixed, jnp.swapaxes(velocities, 0, 1))
    partial = tile_forces(pairs, tile_live, places, fixed)
    forces, arrived = pl.pallas_call(
        last_kernel,
        out_shape=(shape((3, CL, LANES)), shape((ARRIVING, 8, LANES))),
        in_specs=[VMEM] * 5,
        out_specs=(VMEM, VMEM),
        scratch_shapes=[
            landing,
            pltpu.VMEM((ARRIVING, 8, LANES), F32),
            dma(5, 3),
            dma(5, 3),
            dma(TOWERS),
            dma(TOWERS),
            pltpu.SemaphoreType.DMA,
        ],
        compiler_params=params(2),
    )(partial, fixed, places, moving, destinations.T)
    return jnp.swapaxes(forces, 0, 1), arrived


def solution(mesh):
    home = ("gz", "gy", "gx")
    placed = (
        P(home, None, None),
        P(home, None, None),
        P(home, None),
        P(home, None),
        P(),
        P(home, None),
        P(home),
        P(home, None),
    )
    return jax.shard_map(
        local,
        mesh=mesh,
        in_specs=placed,
        out_specs=(P(home, None, None), P(home, None, None)),
        check_vma=False,
    )
```

```python
import functools

import jax
import jax.numpy as jnp
from jax import lax
from jax.experimental import pallas as pl
from jax.experimental.pallas import tpu as pltpu
from jax.sharding import PartitionSpec as P

coulomb = 0.3
time_step = 0.05

MESH = pl.DeviceIdType.MESH
F32 = jnp.float32
BF16 = jnp.bfloat16

CL = 64
LANES = 128
SLOTS = 6
ROWS = SLOTS * CL
CAPACITY = 4
TILES = 256
TOWERS = 32
ARRIVING = TOWERS * CAPACITY
UNROLL = 16
CENTER = 2.0
PLANES = 32
CHANNELS = 8
RADIUS, CHARGE = 3, 4


def split(x):
    high = x.astype(BF16).astype(F32)
    rest = x - high
    middle = rest.astype(BF16).astype(F32)
    return high, middle, rest - middle


def tile_kernel(tiles, live, blocks, out, planes, totals, store_a, store_b):
    line = lax.broadcasted_iota(jnp.int32, (8, LANES), 0)
    upper = line < 4
    center = jnp.where(line < 3, CENTER, 0.0).astype(F32)
    zero = jnp.zeros((8, LANES), F32)

    def prepare(step, carry):
        slot, inner = step // (CL // 8), step % (CL // 8)
        for k in range(8):
            first = pl.multiple_of(slot * (CHANNELS * CL) + inner * 8, 8) + k
            to = pl.multiple_of(step * 256, 256) + k * 32
            loaded = blocks[pl.ds(first, 8, stride=CL), :] - center
            twice = jnp.where(upper, loaded, pltpu.roll(loaded, 4, 0))
            charge = jnp.broadcast_to(loaded[4:5, :], (8, LANES))
            high, middle, low = split(twice)
            planes[pl.ds(to, 8), :] = jnp.where(upper, high, middle)
            planes[pl.ds(to + 8, 8), :] = jnp.where(upper, low, high)
            square = twice * twice
            square = square + pltpu.roll(square, 2, 0)
            square = 0.5 * (square + pltpu.roll(square, 1, 0))
            high, middle, low = split(square)
            parts = jnp.where(line == 0, high, jnp.where(line == 1, middle, low))
            planes[pl.ds(to + 16, 8), :] = jnp.where(line < 3, parts, jnp.where((line == 3) | (line == 7), 0.0, 1.0))
            weighted = jnp.where((line == 3) | (line == 7), 1.0, twice) * charge
            high = weighted.astype(BF16).astype(F32)
            planes[pl.ds(to + 24, 8), :] = jnp.where(upper, high, weighted - high)
            totals[pl.ds(pl.multiple_of(step * 64, 64) + k * 8, 8), :] = zero
        return carry

    lax.fori_loop(0, ROWS // 8, prepare, 0)

    sign = jnp.where(line % 4 == 3, 1.0, -1.0).astype(F32)
    live_count = live[0]

    def eight(plane, row):
        return planes[pl.ds(pl.multiple_of(row * 32, 32) + plane * 8, 8), :]

    blank = jnp.zeros((32, LANES), F32)

    def powers_of(group, pair, store):
        lefts, rights = [], []
        for v in range(2):
            a, b = tiles[0, group * UNROLL + 2 * pair + v], tiles[1, group * UNROLL + 2 * pair + v]
            near = eight(0, a) * sign
            lefts += [near, near, eight(1, a) * sign, eight(2, a)]
            r0, r1, r2 = eight(0, b), eight(1, b), eight(2, b)
            rights.append(
                jnp.concatenate([r0, pltpu.roll(r0, 4, 0), pltpu.roll(r1, 4, 0), pltpu.roll(r2, 4, 0)], axis=0)
            )
        left = jnp.concatenate(lefts, axis=0)
        right = jnp.concatenate(
            [jnp.concatenate([rights[0], blank], axis=1), jnp.concatenate([blank, rights[1]], axis=1)], axis=0
        )
        half_dist = lax.dot_general(
            left.astype(BF16), right.astype(BF16), (((0,), (0,)), ((), ())), preferred_element_type=F32
        )
        root = lax.rsqrt(half_dist)
        power = root * root * root
        high = power.astype(BF16)
        store[pair, 0:128, :] = high
        store[pair, 128:256, :] = (power - high.astype(F32)).astype(BF16)

    def sums_of(group, pair, store, sums):
        ids = [(tiles[0, group * UNROLL + 2 * pair + v], tiles[1, group * UNROLL + 2 * pair + v]) for v in range(2)]
        active = [jnp.where(group * UNROLL + 2 * pair + v < live_count, 1.0, 0.0).astype(F32) for v in range(2)]
        from_a = jnp.concatenate([eight(3, ids[v][0]) * active[v] for v in range(2)], axis=0).astype(BF16)
        from_b = jnp.concatenate([eight(3, ids[v][1]) * active[v] for v in range(2)], axis=0).astype(BF16)
        on_right = jnp.dot(jnp.concatenate([from_a, from_a], axis=1), store[pair], preferred_element_type=F32)
        across = jnp.concatenate(
            [
                jnp.concatenate([store[pair, 0:128, 0:128], store[pair, 128:256, 0:128]], axis=1),
                jnp.concatenate([store[pair, 0:128, 128:256], store[pair, 128:256, 128:256]], axis=1),
            ],
            axis=0,
        )
        on_left = lax.dot_general(
            jnp.concatenate([from_b, from_b], axis=1), across, (((1,), (1,)), ((), ())), preferred_element_type=F32
        )
        sums.append((ids[0][0], on_left[0:8, :LANES]))
        sums.append((ids[0][1], on_right[0:8, :LANES]))
        sums.append((ids[1][0], on_left[8:16, LANES:]))
        sums.append((ids[1][1], on_right[8:16, LANES:]))

    def add(sums):
        for row, value in sums:
            at = pl.ds(pl.multiple_of(row * 8, 8), 8)
            totals[at, :] = totals[at, :] + value

    half_group = UNROLL // 2
    for pair in range(half_group):
        powers_of(0, pair, store_a)

    def two_groups(step, carry):
        group = 2 * step
        for now, later, shift in ((store_a, store_b, 1), (store_b, store_a, 2)):
            sums = []
            for pair in range(half_group):
                powers_of(jnp.minimum(group + shift, TILES // UNROLL - 1), pair, later)
                sums_of(group + shift - 1, pair, now, sums)
            add(sums)
        return carry

    lax.fori_loop(0, (live_count + 2 * UNROLL - 1) // (2 * UNROLL), two_groups, 0)

    factor = coulomb * 0.5**1.5

    def finish(group, carry):
        slot, inner = group // (CL // 8), group % (CL // 8)
        rows = pl.ds(pl.multiple_of(inner * 8, 8), 8)

        def plane(c):
            return blocks[pl.ds(pl.multiple_of(slot * (CHANNELS * CL) + c * CL + inner * 8, 8), 8), :]

        def summed(channel):
            first = pl.multiple_of(group * 64, 64) + channel
            return totals[pl.ds(first, 8, stride=8), :] + totals[pl.ds(first + 4, 8, stride=8), :]

        scale = factor * plane(4)
        whole = summed(3)
        for c in range(3):
            out[slot, c, rows, :] = scale * ((plane(c) - CENTER) * whole - summed(c))
        return carry

    lax.fori_loop(0, ROWS // 8, finish, 0)


def tile_forces(tiles, live, blocks):
    return pl.pallas_call(
        tile_kernel,
        out_shape=jax.ShapeDtypeStruct((SLOTS, 3, CL, LANES), F32),
        in_specs=[
            pl.BlockSpec(memory_space=pltpu.SMEM),
            pl.BlockSpec(memory_space=pltpu.SMEM),
            pl.BlockSpec(memory_space=pltpu.VMEM),
        ],
        out_specs=pl.BlockSpec(memory_space=pltpu.VMEM),
        scratch_shapes=[
            pltpu.VMEM((PLANES * ROWS, LANES), F32),
            pltpu.VMEM((ROWS * 8, LANES), F32),
            pltpu.VMEM((UNROLL // 2, 256, 256), BF16),
            pltpu.VMEM((UNROLL // 2, 256, 256), BF16),
        ],
        compiler_params=pltpu.CompilerParams(vmem_limit_bytes=40 * 2**20),
        cost_estimate=pl.CostEstimate(flops=256 * 128 * 128 * 120, bytes_accessed=2 * 2**20, transcendentals=256 * 128 * 128),
    )(tiles, live, blocks.reshape(SLOTS * CHANNELS * CL, LANES))


VMEM = pl.BlockSpec(memory_space=pltpu.VMEM)
HBM = pl.BlockSpec(memory_space=pltpu.HBM)
SMEM = pl.BlockSpec(memory_space=pltpu.SMEM)
BELOW, ABOVE = 4, 5


def here():
    return lax.axis_index("gz"), lax.axis_index("gy"), lax.axis_index("gx")


def neighbours():
    z, y, x = here()
    even = lax.rem(z, 2) == 0
    step = 1 - 2 * lax.rem(z, 2)
    pair = z + step
    return dict(
        core=(z, 1 - y, x),
        pair=(pair, y, x),
        cross=(pair, y, 1 - x),
        ahead=(lax.rem(z + 2 * step + TOWERS, TOWERS), y, x),
        behind=(lax.rem(z - 2 * step + TOWERS, TOWERS), y, x),
        mine=y * 2 + x,
        core_slot=(1 - y) * 2 + x,
        plate_slot=y * 2 + 1 - x,
        far_slot=(1 - y) * 2 + 1 - x,
        pair_slot=ABOVE - lax.rem(z, 2),
        other_slot=BELOW + lax.rem(z, 2),
    )


PARTNERS = ("core", "pair", "cross", "ahead", "behind")


def greet(devices):
    barrier = pltpu.get_barrier_semaphore()
    for device in devices:
        pl.semaphore_signal(barrier, inc=1, device_id=device, device_id_type=MESH)
    return barrier


def remote(source, target, send_sems, recv_sems, way, chunk, device):
    return pltpu.make_async_remote_copy(
        source, target, send_sems.at[way, chunk], recv_sems.at[way, chunk], device_id=device, device_id_type=MESH
    )


def spread(n, buffer, channels, send_sems, recv_sems, ready):
    sent = []

    def send(way, chunk, slot, there, name):
        copy = remote(buffer.at[slot, chunk], buffer.at[there, chunk], send_sems, recv_sems, way, chunk, n[name])
        copy.start()
        sent.append(copy)

    def arrive(way, chunk, slot):
        remote(buffer.at[slot, chunk], buffer.at[slot, chunk], send_sems, recv_sems, way, chunk, n["core"]).wait_recv()

    for c in channels:
        ready(c)
        send(1, c, n["mine"], n["other_slot"], "pair")
        send(0, c, n["mine"], n["mine"], "core")
    for c in channels:
        arrive(1, c, n["pair_slot"])
        send(2, c, n["pair_slot"], n["mine"], "cross")
        send(3, c, n["pair_slot"], n["other_slot"], "ahead")
    for c in channels:
        arrive(2, c, n["plate_slot"])
        send(4, c, n["plate_slot"], n["plate_slot"], "core")
    for c in channels:
        arrive(0, c, n["core_slot"])
        arrive(3, c, n["other_slot"])
        arrive(4, c, n["far_slot"])
    for copy in sent:
        copy.wait_send()


def gather_forces(n, partial, landing, send_sems, recv_sems):
    sent = []

    def send(way, chunk, source, name):
        copy = remote(source, landing.at[way, chunk], send_sems, recv_sems, way, chunk, n[name])
        copy.start()
        sent.append(copy)

    def arrive(way, chunk):
        place = landing.at[way, chunk]
        remote(place, place, send_sems, recv_sems, way, chunk, n["core"]).wait_recv()

    for c in range(3):
        send(0, c, partial.at[n["far_slot"], c], "core")
        send(2, c, partial.at[n["other_slot"], c], "behind")
    for c in range(3):
        send(4, c, partial.at[n["core_slot"], c], "core")
    for c in range(3):
        arrive(0, c)
        landing[5, c] = partial[n["plate_slot"], c] + landing[0, c]
        send(1, c, landing.at[5, c], "cross")
    for c in range(3):
        arrive(1, c)
        arrive(2, c)
        landing[6, c] = partial[n["pair_slot"], c] + landing[1, c] + landing[2, c]
        send(3, c, landing.at[6, c], "pair")

    def total(c):
        arrive(3, c)
        arrive(4, c)
        return partial[n["mine"], c] + landing[3, c] + landing[4, c]

    return total, sent


def import_kernel(radii, positions, charges, types, buffer, kinds, table, load_sems, send_sems, recv_sems):
    n = neighbours()
    mine = n["mine"]
    loads = [pltpu.make_async_copy(positions.at[c], buffer.at[mine, c], load_sems.at[c]) for c in range(3)]
    loads.append(pltpu.make_async_copy(types, kinds, load_sems.at[3]))
    loads.append(pltpu.make_async_copy(charges, buffer.at[mine, CHARGE], load_sems.at[4]))
    loads.append(pltpu.make_async_copy(radii, table, load_sems.at[5]))
    for load in loads:
        load.start()
    barrier = greet([n[name] for name in PARTNERS])
    pl.semaphore_wait(barrier, len(PARTNERS))

    def ready(c):
        loads[c].wait()
        if c == RADIUS:
            loads[5].wait()
            radius = jnp.zeros((CL, LANES), F32)
            for kind in range(16):
                radius = jnp.where(kinds[...] == kind, table[kind], radius)
            buffer[mine, RADIUS] = radius

    spread(n, buffer, (0, 1, 2, CHARGE, RADIUS), send_sems, recv_sems, ready)


def step_kernel(partial, fixed, velocities, places, moving, landing, send_sems, recv_sems, next_send, next_recv):
    n = neighbours()
    mine = n["mine"]
    barrier = greet([n[name] for name in PARTNERS])
    pl.semaphore_wait(barrier, len(PARTNERS))
    force, sent = gather_forces(n, partial, landing, send_sems, recv_sems)

    def ready(c):
        speed = velocities[c] + time_step * force(c)
        moving[c] = speed
        places[mine, c] = fixed[mine, c] + time_step * speed

    for slot in range(SLOTS):
        for c in (RADIUS, CHARGE):
            places[slot, c] = fixed[slot, c]
    spread(n, places, range(3), next_send, next_recv, ready)
    for copy in sent:
        copy.wait_send()


def last_kernel(
    partial, places, moving, destinations, forces_out, arrived, landing, slots, send_sems, recv_sems, out_sems, in_sems, own_sem
):
    z, y, x = here()
    n = neighbours()
    mine = n["mine"]
    others = [(lax.rem(z + k, TOWERS), y, x) for k in range(1, TOWERS)]
    barrier = greet([n["core"], n["cross"]] + others)

    row = jnp.broadcast_to(destinations[...].astype(F32), (CL, CL))
    r = lax.broadcasted_iota(jnp.int32, (CL, CL), 0)
    c = lax.broadcasted_iota(jnp.int32, (CL, CL), 1)
    column = jnp.sum(jnp.where(r == c, row, 0.0), axis=1, keepdims=True)
    rank = jnp.sum(jnp.where((column == row) & (r < c), 1.0, 0.0), axis=0, keepdims=True)
    slot = row[0:1] * CAPACITY + rank
    select = (lax.broadcasted_iota(jnp.int32, (ARRIVING, CL), 0).astype(F32) == slot).astype(BF16)

    pl.semaphore_wait(barrier, 2 + TOWERS - 1)
    force, sent = gather_forces(n, partial, landing, send_sems, recv_sems)
    carried = []
    speeds = []
    for k in range(3):
        total = force(k)
        forces_out[k] = total
        speed = moving[k] + time_step * total
        speeds.append(speed)
        carried.append(places[mine, k] + time_step * speed)
    carried = carried + speeds + [places[mine, CHARGE], places[mine, RADIUS]]
    for k, value in enumerate(carried):
        parts = split(value)
        slots[:, k, :] = sum(jnp.dot(select, part.astype(BF16), preferred_element_type=F32) for part in reversed(parts))

    def send(tower):
        return pltpu.make_async_remote_copy(
            slots.at[pl.ds(tower * CAPACITY, CAPACITY)],
            arrived.at[pl.ds(z * CAPACITY, CAPACITY)],
            out_sems.at[tower],
            in_sems.at[z],
            device_id=(tower, y, x),
            device_id_type=MESH,
        )

    def receive(tower):
        return pltpu.make_async_remote_copy(
            slots.at[pl.ds(tower * CAPACITY, CAPACITY)],
            arrived.at[pl.ds(tower * CAPACITY, CAPACITY)],
            out_sems.at[tower],
            in_sems.at[tower],
            device_id=(tower, y, x),
            device_id_type=MESH,
        )

    for k in range(1, TOWERS):
        send(lax.rem(z + k, TOWERS)).start()
    own = pltpu.make_async_copy(
        slots.at[pl.ds(z * CAPACITY, CAPACITY)], arrived.at[pl.ds(z * CAPACITY, CAPACITY)], own_sem
    )
    own.start()
    own.wait()
    for k in range(1, TOWERS):
        receive(lax.rem(z + TOWERS - k, TOWERS)).wait_recv()
    for k in range(1, TOWERS):
        send(lax.rem(z + k, TOWERS)).wait_send()
    for copy in sent:
        copy.wait_send()


def params(number):
    return pltpu.CompilerParams(collective_id=number, has_side_effects=True, vmem_limit_bytes=40 * 2**20)


def dma(*counts):
    return pltpu.SemaphoreType.DMA(counts)


def local(positions, velocities, charges, atom_types, type_radius, tiles, tile_live, destinations):
    held = functools.partial(pltpu.with_memory_space_constraint, memory_space=pltpu.HBM)
    shape = functools.partial(jax.ShapeDtypeStruct, dtype=F32)
    pairs = tiles.T
    landing = pltpu.VMEM((7, 3, CL, LANES), F32)
    fixed = pl.pallas_call(
        import_kernel,
        out_shape=shape((SLOTS, CHANNELS, CL, LANES)),
        in_specs=[HBM] * 4,
        out_specs=VMEM,
        scratch_shapes=[pltpu.VMEM((CL, LANES), jnp.int32), pltpu.SMEM((16,), F32), dma(6), dma(5, 5), dma(5, 5)],
        compiler_params=params(0),
    )(*(held(v) for v in (type_radius, jnp.swapaxes(positions, 0, 1), charges, atom_types)))
    partial = tile_forces(pairs, tile_live, fixed)
    places, moving = pl.pallas_call(
        step_kernel,
        out_shape=(shape((SLOTS, CHANNELS, CL, LANES)), shape((3, CL, LANES))),
        in_specs=[VMEM] * 3,
        out_specs=(VMEM, VMEM),
        scratch_shapes=[landing, dma(5, 3), dma(5, 3), dma(5, 3), dma(5, 3)],
        compiler_params=params(1),
    )(partial, fixed, jnp.swapaxes(velocities, 0, 1))
    partial = tile_forces(pairs, tile_live, places)
    forces, arrived = pl.pallas_call(
        last_kernel,
        out_shape=(shape((3, CL, LANES)), shape((ARRIVING, 8, LANES))),
        in_specs=[VMEM] * 4,
        out_specs=(VMEM, VMEM),
        scratch_shapes=[
            landing,
            pltpu.VMEM((ARRIVING, 8, LANES), F32),
            dma(5, 3),
            dma(5, 3),
            dma(TOWERS),
            dma(TOWERS),
            pltpu.SemaphoreType.DMA,
        ],
        compiler_params=params(2),
    )(partial, places, moving, destinations.T)
    return jnp.swapaxes(forces, 0, 1), arrived


def solution(mesh):
    home = ("gz", "gy", "gx")
    placed = (
        P(home, None, None),
        P(home, None, None),
        P(home, None),
        P(home, None),
        P(),
        P(home, None),
        P(home),
        P(home, None),
    )
    return jax.shard_map(
        local,
        mesh=mesh,
        in_specs=placed,
        out_specs=(P(home, None, None), P(home, None, None)),
        check_vma=False,
    )
```

```python
import functools

import jax
import jax.numpy as jnp
from jax import lax
from jax.experimental import pallas as pl
from jax.experimental.pallas import tpu as pltpu
from jax.sharding import PartitionSpec as P

coulomb = 0.3
time_step = 0.05

MESH = pl.DeviceIdType.MESH
F32 = jnp.float32
BF16 = jnp.bfloat16

CL = 64
LANES = 128
SLOTS = 6
ROWS = SLOTS * CL
CAPACITY = 4
TILES = 256
TOWERS = 32
ARRIVING = TOWERS * CAPACITY
UNROLL = 16
CENTER = 2.0
PLANES = 32
CHANNELS = 8
RADIUS, CHARGE = 3, 4


def split(x):
    high = x.astype(BF16).astype(F32)
    rest = x - high
    middle = rest.astype(BF16).astype(F32)
    return high, middle, rest - middle


def tile_kernel(tiles, live, blocks, planes, out, totals, store_a, store_b):
    line = lax.broadcasted_iota(jnp.int32, (8, LANES), 0)

    def clear(step, carry):
        for k in range(8):
            totals[pl.ds(pl.multiple_of(step * 64, 64) + k * 8, 8), :] = jnp.zeros((8, LANES), F32)
        return carry

    lax.fori_loop(0, ROWS // 8, clear, 0)

    sign = jnp.where(line % 4 == 3, 1.0, -1.0).astype(F32)
    live_count = live[0]

    def eight(plane, row):
        return planes[pl.ds(pl.multiple_of(row * 32, 32) + plane * 8, 8), :]

    blank = jnp.zeros((32, LANES), F32)

    def powers_of(group, pair, store):
        lefts, rights = [], []
        for v in range(2):
            a, b = tiles[0, group * UNROLL + 2 * pair + v], tiles[1, group * UNROLL + 2 * pair + v]
            near = eight(0, a) * sign
            lefts += [near, near, eight(1, a) * sign, eight(2, a)]
            r0, r1, r2 = eight(0, b), eight(1, b), eight(2, b)
            rights.append(
                jnp.concatenate([r0, pltpu.roll(r0, 4, 0), pltpu.roll(r1, 4, 0), pltpu.roll(r2, 4, 0)], axis=0)
            )
        left = jnp.concatenate(lefts, axis=0)
        right = jnp.concatenate(
            [jnp.concatenate([rights[0], blank], axis=1), jnp.concatenate([blank, rights[1]], axis=1)], axis=0
        )
        half_dist = lax.dot_general(
            left.astype(BF16), right.astype(BF16), (((0,), (0,)), ((), ())), preferred_element_type=F32
        )
        root = lax.rsqrt(half_dist)
        power = root * root * root
        high = power.astype(BF16)
        store[pair, 0:128, :] = high
        store[pair, 128:256, :] = (power - high.astype(F32)).astype(BF16)

    def sums_of(group, pair, store, sums):
        ids = [(tiles[0, group * UNROLL + 2 * pair + v], tiles[1, group * UNROLL + 2 * pair + v]) for v in range(2)]
        active = [jnp.where(group * UNROLL + 2 * pair + v < live_count, 1.0, 0.0).astype(F32) for v in range(2)]
        from_a = jnp.concatenate([eight(3, ids[v][0]) * active[v] for v in range(2)], axis=0).astype(BF16)
        from_b = jnp.concatenate([eight(3, ids[v][1]) * active[v] for v in range(2)], axis=0).astype(BF16)
        on_right = jnp.dot(jnp.concatenate([from_a, from_a], axis=1), store[pair], preferred_element_type=F32)
        across = jnp.concatenate(
            [
                jnp.concatenate([store[pair, 0:128, 0:128], store[pair, 128:256, 0:128]], axis=1),
                jnp.concatenate([store[pair, 0:128, 128:256], store[pair, 128:256, 128:256]], axis=1),
            ],
            axis=0,
        )
        on_left = lax.dot_general(
            jnp.concatenate([from_b, from_b], axis=1), across, (((1,), (1,)), ((), ())), preferred_element_type=F32
        )
        sums.append((ids[0][0], on_left[0:8, :LANES]))
        sums.append((ids[0][1], on_right[0:8, :LANES]))
        sums.append((ids[1][0], on_left[8:16, LANES:]))
        sums.append((ids[1][1], on_right[8:16, LANES:]))

    def add(sums):
        for row, value in sums:
            at = pl.ds(pl.multiple_of(row * 8, 8), 8)
            totals[at, :] = totals[at, :] + value

    half_group = UNROLL // 2
    for pair in range(half_group):
        powers_of(0, pair, store_a)

    def two_groups(step, carry):
        group = 2 * step
        for now, later, shift in ((store_a, store_b, 1), (store_b, store_a, 2)):
            sums = []
            for pair in range(half_group):
                powers_of(jnp.minimum(group + shift, TILES // UNROLL - 1), pair, later)
                sums_of(group + shift - 1, pair, now, sums)
            add(sums)
        return carry

    lax.fori_loop(0, (live_count + 2 * UNROLL - 1) // (2 * UNROLL), two_groups, 0)

    factor = coulomb * 0.5**1.5

    def finish(group, carry):
        slot, inner = group // (CL // 8), group % (CL // 8)
        rows = pl.ds(pl.multiple_of(inner * 8, 8), 8)

        def plane(c):
            return blocks[pl.ds(pl.multiple_of(slot * (CHANNELS * CL) + c * CL + inner * 8, 8), 8), :]

        def summed(channel):
            first = pl.multiple_of(group * 64, 64) + channel
            return totals[pl.ds(first, 8, stride=8), :] + totals[pl.ds(first + 4, 8, stride=8), :]

        scale = factor * plane(4)
        whole = summed(3)
        for c in range(3):
            out[slot, c, rows, :] = scale * ((plane(c) - CENTER) * whole - summed(c))
        return carry

    lax.fori_loop(0, ROWS // 8, finish, 0)


def tile_forces(tiles, live, blocks, planes):
    return pl.pallas_call(
        tile_kernel,
        out_shape=jax.ShapeDtypeStruct((SLOTS, 3, CL, LANES), F32),
        in_specs=[
            pl.BlockSpec(memory_space=pltpu.SMEM),
            pl.BlockSpec(memory_space=pltpu.SMEM),
            pl.BlockSpec(memory_space=pltpu.VMEM),
            pl.BlockSpec(memory_space=pltpu.VMEM),
        ],
        out_specs=pl.BlockSpec(memory_space=pltpu.VMEM),
        scratch_shapes=[
            pltpu.VMEM((ROWS * 8, LANES), F32),
            pltpu.VMEM((UNROLL // 2, 256, 256), BF16),
            pltpu.VMEM((UNROLL // 2, 256, 256), BF16),
        ],
        compiler_params=pltpu.CompilerParams(vmem_limit_bytes=40 * 2**20),
        cost_estimate=pl.CostEstimate(flops=256 * 128 * 128 * 120, bytes_accessed=2 * 2**20, transcendentals=256 * 128 * 128),
    )(tiles, live, blocks, planes)


VMEM = pl.BlockSpec(memory_space=pltpu.VMEM)
HBM = pl.BlockSpec(memory_space=pltpu.HBM)
SMEM = pl.BlockSpec(memory_space=pltpu.SMEM)
BELOW, ABOVE = 4, 5


def here():
    return lax.axis_index("gz"), lax.axis_index("gy"), lax.axis_index("gx")


def neighbours():
    z, y, x = here()
    even = lax.rem(z, 2) == 0
    step = 1 - 2 * lax.rem(z, 2)
    pair = z + step
    return dict(
        core=(z, 1 - y, x),
        pair=(pair, y, x),
        cross=(pair, y, 1 - x),
        ahead=(lax.rem(z + 2 * step + TOWERS, TOWERS), y, x),
        behind=(lax.rem(z - 2 * step + TOWERS, TOWERS), y, x),
        mine=y * 2 + x,
        core_slot=(1 - y) * 2 + x,
        plate_slot=y * 2 + 1 - x,
        far_slot=(1 - y) * 2 + 1 - x,
        pair_slot=ABOVE - lax.rem(z, 2),
        other_slot=BELOW + lax.rem(z, 2),
    )


PARTNERS = ("core", "pair", "cross", "ahead", "behind")


def greet(devices):
    barrier = pltpu.get_barrier_semaphore()
    for device in devices:
        pl.semaphore_signal(barrier, inc=1, device_id=device, device_id_type=MESH)
    return barrier


def channel(slot, c):
    return pl.ds(pl.multiple_of(slot * (CHANNELS * CL) + c * CL, CL), CL)


def prepare(slot, blocks, planes):
    line = lax.broadcasted_iota(jnp.int32, (8, LANES), 0)
    upper = line < 4
    center = jnp.where(line < 3, CENTER, 0.0).astype(F32)

    def eight_clusters(step, carry):
        for k in range(8):
            first = pl.multiple_of(slot * (CHANNELS * CL) + step * 8, 8) + k
            to = pl.multiple_of(slot * (CL * PLANES) + step * (8 * PLANES), 8 * PLANES) + k * PLANES
            loaded = blocks[pl.ds(first, 8, stride=CL), :] - center
            twice = jnp.where(upper, loaded, pltpu.roll(loaded, 4, 0))
            charge = jnp.broadcast_to(loaded[4:5, :], (8, LANES))
            high, middle, low = split(twice)
            planes[pl.ds(to, 8), :] = jnp.where(upper, high, middle)
            planes[pl.ds(to + 8, 8), :] = jnp.where(upper, low, high)
            square = twice * twice
            square = square + pltpu.roll(square, 2, 0)
            square = 0.5 * (square + pltpu.roll(square, 1, 0))
            high, middle, low = split(square)
            parts = jnp.where(line == 0, high, jnp.where(line == 1, middle, low))
            planes[pl.ds(to + 16, 8), :] = jnp.where(line < 3, parts, jnp.where((line == 3) | (line == 7), 0.0, 1.0))
            weighted = jnp.where((line == 3) | (line == 7), 1.0, twice) * charge
            high = weighted.astype(BF16).astype(F32)
            planes[pl.ds(to + 24, 8), :] = jnp.where(upper, high, weighted - high)
        return carry

    lax.fori_loop(0, CL // 8, eight_clusters, 0)


def clear_unused(blocks):
    for slot in range(SLOTS):
        for c in range(5, CHANNELS):
            blocks[channel(slot, c), :] = jnp.zeros((CL, LANES), F32)


def remote(source, target, send_sems, recv_sems, way, chunk, device):
    return pltpu.make_async_remote_copy(
        source, target, send_sems.at[way, chunk], recv_sems.at[way, chunk], device_id=device, device_id_type=MESH
    )


def spread(n, buffer, planes, channels, send_sems, recv_sems, ready):
    sent = []

    def send(way, chunk, slot, there, name):
        copy = remote(buffer.at[channel(slot, chunk)], buffer.at[channel(there, chunk)], send_sems, recv_sems, way, chunk, n[name])
        copy.start()
        sent.append(copy)

    def arrive(way, chunk, slot):
        place = buffer.at[channel(slot, chunk)]
        remote(place, place, send_sems, recv_sems, way, chunk, n["core"]).wait_recv()

    for c in channels:
        ready(c)
        send(1, c, n["mine"], n["other_slot"], "pair")
        send(0, c, n["mine"], n["mine"], "core")
    prepare(n["mine"], buffer, planes)
    for c in channels:
        arrive(1, c, n["pair_slot"])
        send(2, c, n["pair_slot"], n["mine"], "cross")
        send(3, c, n["pair_slot"], n["other_slot"], "ahead")
    prepare(n["pair_slot"], buffer, planes)
    for c in channels:
        arrive(0, c, n["core_slot"])
    prepare(n["core_slot"], buffer, planes)
    for c in channels:
        arrive(2, c, n["plate_slot"])
        send(4, c, n["plate_slot"], n["plate_slot"], "core")
    prepare(n["plate_slot"], buffer, planes)
    for c in channels:
        arrive(4, c, n["far_slot"])
    prepare(n["far_slot"], buffer, planes)
    for c in channels:
        arrive(3, c, n["other_slot"])
    prepare(n["other_slot"], buffer, planes)
    for copy in sent:
        copy.wait_send()


def gather_forces(n, partial, landing, send_sems, recv_sems, meanwhile):
    sent = []

    def send(way, chunk, source, name):
        copy = remote(source, landing.at[way, chunk], send_sems, recv_sems, way, chunk, n[name])
        copy.start()
        sent.append(copy)

    def arrive(way, chunk):
        place = landing.at[way, chunk]
        remote(place, place, send_sems, recv_sems, way, chunk, n["core"]).wait_recv()

    for c in range(3):
        send(0, c, partial.at[n["far_slot"], c], "core")
        send(2, c, partial.at[n["other_slot"], c], "behind")
    for c in range(3):
        send(4, c, partial.at[n["core_slot"], c], "core")
    meanwhile()
    for c in range(3):
        arrive(0, c)
        landing[5, c] = partial[n["plate_slot"], c] + landing[0, c]
        send(1, c, landing.at[5, c], "cross")
    for c in range(3):
        arrive(1, c)
        arrive(2, c)
        landing[6, c] = partial[n["pair_slot"], c] + landing[1, c] + landing[2, c]
        send(3, c, landing.at[6, c], "pair")

    def total(c):
        arrive(3, c)
        arrive(4, c)
        return partial[n["mine"], c] + landing[3, c] + landing[4, c]

    return total, sent


def import_kernel(radii, positions, charges, types, buffer, planes, kinds, table, load_sems, send_sems, recv_sems):
    n = neighbours()
    mine = n["mine"]
    loads = [pltpu.make_async_copy(positions.at[c], buffer.at[channel(mine, c)], load_sems.at[c]) for c in range(3)]
    loads.append(pltpu.make_async_copy(types, kinds, load_sems.at[3]))
    loads.append(pltpu.make_async_copy(charges, buffer.at[channel(mine, CHARGE)], load_sems.at[4]))
    loads.append(pltpu.make_async_copy(radii, table, load_sems.at[5]))
    for load in loads:
        load.start()
    barrier = greet([n[name] for name in PARTNERS])
    clear_unused(buffer)
    pl.semaphore_wait(barrier, len(PARTNERS))

    def ready(c):
        loads[c].wait()
        if c == RADIUS:
            loads[5].wait()
            radius = jnp.zeros((CL, LANES), F32)
            for kind in range(16):
                radius = jnp.where(kinds[...] == kind, table[kind], radius)
            buffer[channel(mine, RADIUS), :] = radius

    spread(n, buffer, planes, (0, 1, 2, CHARGE, RADIUS), send_sems, recv_sems, ready)


def step_kernel(partial, fixed, velocities, places, planes, moving, landing, send_sems, recv_sems, next_send, next_recv):
    n = neighbours()
    mine = n["mine"]
    barrier = greet([n[name] for name in PARTNERS])
    pl.semaphore_wait(barrier, len(PARTNERS))
    def meanwhile():
        for slot in range(SLOTS):
            for c in (RADIUS, CHARGE):
                places[channel(slot, c), :] = fixed[channel(slot, c), :]
        clear_unused(places)

    force, sent = gather_forces(n, partial, landing, send_sems, recv_sems, meanwhile)

    def ready(c):
        speed = velocities[c] + time_step * force(c)
        moving[c] = speed
        places[channel(mine, c), :] = fixed[channel(mine, c), :] + time_step * speed

    spread(n, places, planes, range(3), next_send, next_recv, ready)
    for copy in sent:
        copy.wait_send()


def last_kernel(
    partial, places, moving, destinations, forces_out, arrived, landing, slots, send_sems, recv_sems, out_sems, in_sems, own_sem
):
    z, y, x = here()
    n = neighbours()
    mine = n["mine"]
    others = [(lax.rem(z + k, TOWERS), y, x) for k in range(1, TOWERS)]
    barrier = greet([n["core"], n["cross"]] + others)

    row = jnp.broadcast_to(destinations[...].astype(F32), (CL, CL))
    r = lax.broadcasted_iota(jnp.int32, (CL, CL), 0)
    c = lax.broadcasted_iota(jnp.int32, (CL, CL), 1)
    column = jnp.sum(jnp.where(r == c, row, 0.0), axis=1, keepdims=True)
    rank = jnp.sum(jnp.where((column == row) & (r < c), 1.0, 0.0), axis=0, keepdims=True)
    slot = row[0:1] * CAPACITY + rank
    select = (lax.broadcasted_iota(jnp.int32, (ARRIVING, CL), 0).astype(F32) == slot).astype(BF16)

    pl.semaphore_wait(barrier, 2 + TOWERS - 1)
    def keep(k, value):
        parts = split(value)
        slots[:, k, :] = sum(jnp.dot(select, part.astype(BF16), preferred_element_type=F32) for part in reversed(parts))

    def meanwhile():
        keep(6, places[channel(mine, CHARGE), :])
        keep(7, places[channel(mine, RADIUS), :])

    force, sent = gather_forces(n, partial, landing, send_sems, recv_sems, meanwhile)
    for k in range(3):
        total = force(k)
        forces_out[k] = total
        speed = moving[k] + time_step * total
        keep(3 + k, speed)
        keep(k, places[channel(mine, k), :] + time_step * speed)

    def send(tower):
        return pltpu.make_async_remote_copy(
            slots.at[pl.ds(tower * CAPACITY, CAPACITY)],
            arrived.at[pl.ds(z * CAPACITY, CAPACITY)],
            out_sems.at[tower],
            in_sems.at[z],
            device_id=(tower, y, x),
            device_id_type=MESH,
        )

    def receive(tower):
        return pltpu.make_async_remote_copy(
            slots.at[pl.ds(tower * CAPACITY, CAPACITY)],
            arrived.at[pl.ds(tower * CAPACITY, CAPACITY)],
            out_sems.at[tower],
            in_sems.at[tower],
            device_id=(tower, y, x),
            device_id_type=MESH,
        )

    for k in range(1, TOWERS):
        send(lax.rem(z + k, TOWERS)).start()
    own = pltpu.make_async_copy(
        slots.at[pl.ds(z * CAPACITY, CAPACITY)], arrived.at[pl.ds(z * CAPACITY, CAPACITY)], own_sem
    )
    own.start()
    own.wait()
    for k in range(1, TOWERS):
        receive(lax.rem(z + TOWERS - k, TOWERS)).wait_recv()
    for k in range(1, TOWERS):
        send(lax.rem(z + k, TOWERS)).wait_send()
    for copy in sent:
        copy.wait_send()


def params(number):
    return pltpu.CompilerParams(collective_id=number, has_side_effects=True, vmem_limit_bytes=40 * 2**20)


def dma(*counts):
    return pltpu.SemaphoreType.DMA(counts)


def local(positions, velocities, charges, atom_types, type_radius, tiles, tile_live, destinations):
    held = functools.partial(pltpu.with_memory_space_constraint, memory_space=pltpu.HBM)
    shape = functools.partial(jax.ShapeDtypeStruct, dtype=F32)
    pairs = tiles.T
    blocks = shape((SLOTS * CHANNELS * CL, LANES))
    operands = shape((ROWS * PLANES, LANES))
    landing = pltpu.VMEM((7, 3, CL, LANES), F32)
    fixed, planes = pl.pallas_call(
        import_kernel,
        out_shape=(blocks, operands),
        in_specs=[HBM] * 4,
        out_specs=(VMEM, VMEM),
        scratch_shapes=[pltpu.VMEM((CL, LANES), jnp.int32), pltpu.SMEM((16,), F32), dma(6), dma(5, 5), dma(5, 5)],
        compiler_params=params(0),
    )(*(held(v) for v in (type_radius, jnp.swapaxes(positions, 0, 1), charges, atom_types)))
    partial = tile_forces(pairs, tile_live, fixed, planes)
    places, planes, moving = pl.pallas_call(
        step_kernel,
        out_shape=(blocks, operands, shape((3, CL, LANES))),
        in_specs=[VMEM] * 3,
        out_specs=(VMEM, VMEM, VMEM),
        scratch_shapes=[landing, dma(5, 3), dma(5, 3), dma(5, 3), dma(5, 3)],
        compiler_params=params(1),
    )(partial, fixed, jnp.swapaxes(velocities, 0, 1))
    partial = tile_forces(pairs, tile_live, places, planes)
    forces, arrived = pl.pallas_call(
        last_kernel,
        out_shape=(shape((3, CL, LANES)), shape((ARRIVING, 8, LANES))),
        in_specs=[VMEM] * 4,
        out_specs=(VMEM, VMEM),
        scratch_shapes=[
            landing,
            pltpu.VMEM((ARRIVING, 8, LANES), F32),
            dma(5, 3),
            dma(5, 3),
            dma(TOWERS),
            dma(TOWERS),
            pltpu.SemaphoreType.DMA,
        ],
        compiler_params=params(2),
    )(partial, places, moving, destinations.T)
    return jnp.swapaxes(forces, 0, 1), arrived


def solution(mesh):
    home = ("gz", "gy", "gx")
    placed = (
        P(home, None, None),
        P(home, None, None),
        P(home, None),
        P(home, None),
        P(),
        P(home, None),
        P(home),
        P(home, None),
    )
    return jax.shard_map(
        local,
        mesh=mesh,
        in_specs=placed,
        out_specs=(P(home, None, None), P(home, None, None)),
        check_vma=False,
    )
```

```python
import functools

import jax
import jax.numpy as jnp
from jax import lax
from jax.experimental import pallas as pl
from jax.experimental.pallas import tpu as pltpu
from jax.sharding import PartitionSpec as P

coulomb = 0.3
time_step = 0.05

MESH = pl.DeviceIdType.MESH
F32 = jnp.float32
BF16 = jnp.bfloat16

CL = 64
LANES = 128
SLOTS = 6
ROWS = SLOTS * CL
CAPACITY = 4
TILES = 256
TOWERS = 32
ARRIVING = TOWERS * CAPACITY
UNROLL = 16
CENTER = 2.0
PLANES = 32
CHANNELS = 8
RADIUS, CHARGE = 3, 4


def split(x):
    high = x.astype(BF16).astype(F32)
    rest = x - high
    middle = rest.astype(BF16).astype(F32)
    return high, middle, rest - middle


def tile_kernel(tiles, live, planes, totals, store_a, store_b):
    line = lax.broadcasted_iota(jnp.int32, (8, LANES), 0)

    def clear(step, carry):
        for k in range(8):
            totals[pl.ds(pl.multiple_of(step * 64, 64) + k * 8, 8), :] = jnp.zeros((8, LANES), F32)
        return carry

    lax.fori_loop(0, ROWS // 8, clear, 0)

    sign = jnp.where(line % 4 == 3, 1.0, -1.0).astype(F32)
    live_count = live[0]

    def eight(plane, row):
        return planes[pl.ds(pl.multiple_of(row * 32, 32) + plane * 8, 8), :]

    blank = jnp.zeros((32, LANES), F32)

    def powers_of(group, pair, store):
        lefts, rights = [], []
        for v in range(2):
            a, b = tiles[0, group * UNROLL + 2 * pair + v], tiles[1, group * UNROLL + 2 * pair + v]
            near = eight(0, a) * sign
            lefts += [near, near, eight(1, a) * sign, eight(2, a)]
            r0, r1, r2 = eight(0, b), eight(1, b), eight(2, b)
            rights.append(
                jnp.concatenate([r0, pltpu.roll(r0, 4, 0), pltpu.roll(r1, 4, 0), pltpu.roll(r2, 4, 0)], axis=0)
            )
        left = jnp.concatenate(lefts, axis=0)
        right = jnp.concatenate(
            [jnp.concatenate([rights[0], blank], axis=1), jnp.concatenate([blank, rights[1]], axis=1)], axis=0
        )
        half_dist = lax.dot_general(
            left.astype(BF16), right.astype(BF16), (((0,), (0,)), ((), ())), preferred_element_type=F32
        )
        root = lax.rsqrt(half_dist)
        power = root * root * root
        high = power.astype(BF16)
        store[pair, 0:128, :] = high
        store[pair, 128:256, :] = (power - high.astype(F32)).astype(BF16)

    def sums_of(group, pair, store, sums):
        ids = [(tiles[0, group * UNROLL + 2 * pair + v], tiles[1, group * UNROLL + 2 * pair + v]) for v in range(2)]
        active = [jnp.where(group * UNROLL + 2 * pair + v < live_count, 1.0, 0.0).astype(F32) for v in range(2)]
        from_a = jnp.concatenate([eight(3, ids[v][0]) * active[v] for v in range(2)], axis=0).astype(BF16)
        from_b = jnp.concatenate([eight(3, ids[v][1]) * active[v] for v in range(2)], axis=0).astype(BF16)
        on_right = jnp.dot(jnp.concatenate([from_a, from_a], axis=1), store[pair], preferred_element_type=F32)
        across = jnp.concatenate(
            [
                jnp.concatenate([store[pair, 0:128, 0:128], store[pair, 128:256, 0:128]], axis=1),
                jnp.concatenate([store[pair, 0:128, 128:256], store[pair, 128:256, 128:256]], axis=1),
            ],
            axis=0,
        )
        on_left = lax.dot_general(
            jnp.concatenate([from_b, from_b], axis=1), across, (((1,), (1,)), ((), ())), preferred_element_type=F32
        )
        sums.append((ids[0][0], on_left[0:8, :LANES]))
        sums.append((ids[0][1], on_right[0:8, :LANES]))
        sums.append((ids[1][0], on_left[8:16, LANES:]))
        sums.append((ids[1][1], on_right[8:16, LANES:]))

    def add(sums):
        for row, value in sums:
            at = pl.ds(pl.multiple_of(row * 8, 8), 8)
            totals[at, :] = totals[at, :] + value

    half_group = UNROLL // 2
    for pair in range(half_group):
        powers_of(0, pair, store_a)

    def two_groups(step, carry):
        group = 2 * step
        for now, later, shift in ((store_a, store_b, 1), (store_b, store_a, 2)):
            sums = []
            for pair in range(half_group):
                sums_of(group + shift - 1, pair, now, sums)
                powers_of(jnp.minimum(group + shift, TILES // UNROLL - 1), pair, later)
            add(sums)
        return carry

    lax.fori_loop(0, (live_count + 2 * UNROLL - 1) // (2 * UNROLL), two_groups, 0)


def tile_forces(tiles, live, planes):
    return pl.pallas_call(
        tile_kernel,
        out_shape=jax.ShapeDtypeStruct((ROWS * 8, LANES), F32),
        in_specs=[
            pl.BlockSpec(memory_space=pltpu.SMEM),
            pl.BlockSpec(memory_space=pltpu.SMEM),
            pl.BlockSpec(memory_space=pltpu.VMEM),
        ],
        out_specs=pl.BlockSpec(memory_space=pltpu.VMEM),
        scratch_shapes=[
            pltpu.VMEM((UNROLL // 2, 256, 256), BF16),
            pltpu.VMEM((UNROLL // 2, 256, 256), BF16),
        ],
        compiler_params=pltpu.CompilerParams(vmem_limit_bytes=40 * 2**20),
        cost_estimate=pl.CostEstimate(flops=256 * 128 * 128 * 120, bytes_accessed=2 * 2**20, transcendentals=256 * 128 * 128),
    )(tiles, live, planes)


VMEM = pl.BlockSpec(memory_space=pltpu.VMEM)
HBM = pl.BlockSpec(memory_space=pltpu.HBM)
SMEM = pl.BlockSpec(memory_space=pltpu.SMEM)
BELOW, ABOVE = 4, 5


def here():
    return lax.axis_index("gz"), lax.axis_index("gy"), lax.axis_index("gx")


def neighbours():
    z, y, x = here()
    even = lax.rem(z, 2) == 0
    step = 1 - 2 * lax.rem(z, 2)
    pair = z + step
    return dict(
        core=(z, 1 - y, x),
        pair=(pair, y, x),
        cross=(pair, y, 1 - x),
        ahead=(lax.rem(z + 2 * step + TOWERS, TOWERS), y, x),
        behind=(lax.rem(z - 2 * step + TOWERS, TOWERS), y, x),
        mine=y * 2 + x,
        core_slot=(1 - y) * 2 + x,
        plate_slot=y * 2 + 1 - x,
        far_slot=(1 - y) * 2 + 1 - x,
        pair_slot=ABOVE - lax.rem(z, 2),
        other_slot=BELOW + lax.rem(z, 2),
    )


PARTNERS = ("core", "pair", "cross", "ahead", "behind")


def greet(devices):
    barrier = pltpu.get_barrier_semaphore()
    for device in devices:
        pl.semaphore_signal(barrier, inc=1, device_id=device, device_id_type=MESH)
    return barrier


def channel(slot, c):
    return pl.ds(pl.multiple_of(slot * (CHANNELS * CL) + c * CL, CL), CL)


def prepare(slot, blocks, planes):
    line = lax.broadcasted_iota(jnp.int32, (8, LANES), 0)
    upper = line < 4
    center = jnp.where(line < 3, CENTER, 0.0).astype(F32)

    def eight_clusters(step, carry):
        for k in range(8):
            first = pl.multiple_of(slot * (CHANNELS * CL) + step * 8, 8) + k
            to = pl.multiple_of(slot * (CL * PLANES) + step * (8 * PLANES), 8 * PLANES) + k * PLANES
            loaded = blocks[pl.ds(first, 8, stride=CL), :] - center
            twice = jnp.where(upper, loaded, pltpu.roll(loaded, 4, 0))
            charge = jnp.broadcast_to(loaded[4:5, :], (8, LANES))
            high, middle, low = split(twice)
            planes[pl.ds(to, 8), :] = jnp.where(upper, high, middle)
            planes[pl.ds(to + 8, 8), :] = jnp.where(upper, low, high)
            square = twice * twice
            square = square + pltpu.roll(square, 2, 0)
            square = 0.5 * (square + pltpu.roll(square, 1, 0))
            high, middle, low = split(square)
            parts = jnp.where(line == 0, high, jnp.where(line == 1, middle, low))
            planes[pl.ds(to + 16, 8), :] = jnp.where(line < 3, parts, jnp.where((line == 3) | (line == 7), 0.0, 1.0))
            weighted = jnp.where((line == 3) | (line == 7), 1.0, twice) * charge
            high = weighted.astype(BF16).astype(F32)
            planes[pl.ds(to + 24, 8), :] = jnp.where(upper, high, weighted - high)
        return carry

    lax.fori_loop(0, CL // 8, eight_clusters, 0)


def finish(slot, totals, blocks, partial):
    factor = coulomb * 0.5**1.5

    def eight_clusters(step, carry):
        rows = pl.ds(pl.multiple_of(step * 8, 8), 8)

        def plane(c):
            return blocks[pl.ds(pl.multiple_of(slot * (CHANNELS * CL) + c * CL + step * 8, 8), 8), :]

        def summed(k):
            first = pl.multiple_of(slot * (CL * 8) + step * 64, 64) + k
            return totals[pl.ds(first, 8, stride=8), :] + totals[pl.ds(first + 4, 8, stride=8), :]

        scale = factor * plane(CHARGE)
        whole = summed(3)
        for c in range(3):
            partial[slot, c, rows, :] = scale * ((plane(c) - CENTER) * whole - summed(c))
        return carry

    lax.fori_loop(0, CL // 8, eight_clusters, 0)


def clear_unused(blocks):
    for slot in range(SLOTS):
        for c in range(5, CHANNELS):
            blocks[channel(slot, c), :] = jnp.zeros((CL, LANES), F32)


def remote(source, target, send_sems, recv_sems, way, chunk, device):
    return pltpu.make_async_remote_copy(
        source, target, send_sems.at[way, chunk], recv_sems.at[way, chunk], device_id=device, device_id_type=MESH
    )


def spread(n, buffer, planes, channels, send_sems, recv_sems, ready):
    sent = []

    def send(way, chunk, slot, there, name):
        copy = remote(buffer.at[channel(slot, chunk)], buffer.at[channel(there, chunk)], send_sems, recv_sems, way, chunk, n[name])
        copy.start()
        sent.append(copy)

    def arrive(way, chunk, slot):
        place = buffer.at[channel(slot, chunk)]
        remote(place, place, send_sems, recv_sems, way, chunk, n["core"]).wait_recv()

    for c in channels:
        ready(c)
        send(1, c, n["mine"], n["other_slot"], "pair")
        send(0, c, n["mine"], n["mine"], "core")
    prepare(n["mine"], buffer, planes)
    for c in channels:
        arrive(1, c, n["pair_slot"])
        send(2, c, n["pair_slot"], n["mine"], "cross")
        send(3, c, n["pair_slot"], n["other_slot"], "ahead")
    prepare(n["pair_slot"], buffer, planes)
    for c in channels:
        arrive(0, c, n["core_slot"])
    prepare(n["core_slot"], buffer, planes)
    for c in channels:
        arrive(2, c, n["plate_slot"])
        send(4, c, n["plate_slot"], n["plate_slot"], "core")
    prepare(n["plate_slot"], buffer, planes)
    for c in channels:
        arrive(4, c, n["far_slot"])
    prepare(n["far_slot"], buffer, planes)
    for c in channels:
        arrive(3, c, n["other_slot"])
    prepare(n["other_slot"], buffer, planes)
    for copy in sent:
        copy.wait_send()


def gather_forces(n, totals, blocks, partial, landing, send_sems, recv_sems, meanwhile):
    sent = []

    def send(way, chunk, source, name):
        copy = remote(source, landing.at[way, chunk], send_sems, recv_sems, way, chunk, n[name])
        copy.start()
        sent.append(copy)

    def arrive(way, chunk):
        place = landing.at[way, chunk]
        remote(place, place, send_sems, recv_sems, way, chunk, n["core"]).wait_recv()

    for way, slot, name in ((0, "far_slot", "core"), (2, "other_slot", "behind"), (4, "core_slot", "core")):
        finish(n[slot], totals, blocks, partial)
        for c in range(3):
            send(way, c, partial.at[n[slot], c], name)
    for slot in ("plate_slot", "pair_slot", "mine"):
        finish(n[slot], totals, blocks, partial)
    meanwhile()
    for c in range(3):
        arrive(0, c)
        landing[5, c] = partial[n["plate_slot"], c] + landing[0, c]
        send(1, c, landing.at[5, c], "cross")
    for c in range(3):
        arrive(1, c)
        arrive(2, c)
        landing[6, c] = partial[n["pair_slot"], c] + landing[1, c] + landing[2, c]
        send(3, c, landing.at[6, c], "pair")

    def total(c):
        arrive(3, c)
        arrive(4, c)
        return partial[n["mine"], c] + landing[3, c] + landing[4, c]

    return total, sent


def import_kernel(radii, positions, charges, types, tiles, buffer, planes, pairs, kinds, table, load_sems, send_sems, recv_sems):
    n = neighbours()
    mine = n["mine"]
    loads = [pltpu.make_async_copy(positions.at[c], buffer.at[channel(mine, c)], load_sems.at[c]) for c in range(3)]
    loads.append(pltpu.make_async_copy(types, kinds, load_sems.at[3]))
    loads.append(pltpu.make_async_copy(charges, buffer.at[channel(mine, CHARGE)], load_sems.at[4]))
    loads.append(pltpu.make_async_copy(radii, table, load_sems.at[5]))
    loads.append(pltpu.make_async_copy(tiles, pairs, load_sems.at[6]))
    for load in loads:
        load.start()
    barrier = greet([n[name] for name in PARTNERS])
    clear_unused(buffer)
    pl.semaphore_wait(barrier, len(PARTNERS))

    def ready(c):
        loads[c].wait()
        if c == RADIUS:
            loads[5].wait()
            radius = jnp.zeros((CL, LANES), F32)
            for kind in range(16):
                radius = jnp.where(kinds[...] == kind, table[kind], radius)
            buffer[channel(mine, RADIUS), :] = radius
            loads[6].wait()

    spread(n, buffer, planes, (0, 1, 2, CHARGE, RADIUS), send_sems, recv_sems, ready)


def step_kernel(totals, fixed, velocities, places, planes, moving, partial, landing, send_sems, recv_sems, next_send, next_recv):
    n = neighbours()
    mine = n["mine"]
    barrier = greet([n[name] for name in PARTNERS])
    pl.semaphore_wait(barrier, len(PARTNERS))
    def meanwhile():
        for slot in range(SLOTS):
            for c in (RADIUS, CHARGE):
                places[channel(slot, c), :] = fixed[channel(slot, c), :]
        clear_unused(places)

    force, sent = gather_forces(n, totals, fixed, partial, landing, send_sems, recv_sems, meanwhile)

    def ready(c):
        speed = velocities[c] + time_step * force(c)
        moving[c] = speed
        places[channel(mine, c), :] = fixed[channel(mine, c), :] + time_step * speed

    spread(n, places, planes, range(3), next_send, next_recv, ready)
    for copy in sent:
        copy.wait_send()


def links(k):
    return min(k // 8, 4 - k // 8) + min(k // 2 % 4, 4 - k // 2 % 4) + k % 2


def last_kernel(
    totals, places, moving, destinations, forces_out, arrived, partial, landing, slots, send_sems, recv_sems, out_sems, in_sems, own_sem
):
    z, y, x = here()
    n = neighbours()
    mine = n["mine"]
    others = [(lax.rem(z + k, TOWERS), y, x) for k in range(1, TOWERS)]
    barrier = greet([n["core"], n["cross"]] + others)

    row = jnp.broadcast_to(destinations[...].astype(F32), (CL, CL))
    r = lax.broadcasted_iota(jnp.int32, (CL, CL), 0)
    c = lax.broadcasted_iota(jnp.int32, (CL, CL), 1)
    column = jnp.sum(jnp.where(r == c, row, 0.0), axis=1, keepdims=True)
    rank = jnp.sum(jnp.where((column == row) & (r < c), 1.0, 0.0), axis=0, keepdims=True)
    slot = row[0:1] * CAPACITY + rank
    select = (lax.broadcasted_iota(jnp.int32, (ARRIVING, CL), 0).astype(F32) == slot).astype(BF16)

    pl.semaphore_wait(barrier, 2 + TOWERS - 1)
    def keep(k, value):
        parts = split(value)
        slots[:, k, :] = sum(jnp.dot(select, part.astype(BF16), preferred_element_type=F32) for part in reversed(parts))

    def meanwhile():
        keep(6, places[channel(mine, CHARGE), :])
        keep(7, places[channel(mine, RADIUS), :])

    force, sent = gather_forces(n, totals, places, partial, landing, send_sems, recv_sems, meanwhile)
    for k in range(3):
        total = force(k)
        forces_out[k] = total
        speed = moving[k] + time_step * total
        keep(3 + k, speed)
        keep(k, places[channel(mine, k), :] + time_step * speed)

    def send(tower):
        return pltpu.make_async_remote_copy(
            slots.at[pl.ds(tower * CAPACITY, CAPACITY)],
            arrived.at[pl.ds(z * CAPACITY, CAPACITY)],
            out_sems.at[tower],
            in_sems.at[z],
            device_id=(tower, y, x),
            device_id_type=MESH,
        )

    def receive(tower):
        return pltpu.make_async_remote_copy(
            slots.at[pl.ds(tower * CAPACITY, CAPACITY)],
            arrived.at[pl.ds(tower * CAPACITY, CAPACITY)],
            out_sems.at[tower],
            in_sems.at[tower],
            device_id=(tower, y, x),
            device_id_type=MESH,
        )

    for k in sorted(range(1, TOWERS), key=links, reverse=True):
        send(lax.rem(z + k, TOWERS)).start()
    own = pltpu.make_async_copy(
        slots.at[pl.ds(z * CAPACITY, CAPACITY)], arrived.at[pl.ds(z * CAPACITY, CAPACITY)], own_sem
    )
    own.start()
    own.wait()
    for k in range(1, TOWERS):
        receive(lax.rem(z + TOWERS - k, TOWERS)).wait_recv()
    for k in range(1, TOWERS):
        send(lax.rem(z + k, TOWERS)).wait_send()
    for copy in sent:
        copy.wait_send()


def params(number):
    return pltpu.CompilerParams(collective_id=number, has_side_effects=True, vmem_limit_bytes=40 * 2**20)


def dma(*counts):
    return pltpu.SemaphoreType.DMA(counts)


def local(positions, velocities, charges, atom_types, type_radius, tiles, tile_live, destinations):
    held = functools.partial(pltpu.with_memory_space_constraint, memory_space=pltpu.HBM)
    shape = functools.partial(jax.ShapeDtypeStruct, dtype=F32)
    blocks = shape((SLOTS * CHANNELS * CL, LANES))
    operands = shape((ROWS * PLANES, LANES))
    partial = pltpu.VMEM((SLOTS, 3, CL, LANES), F32)
    landing = pltpu.VMEM((7, 3, CL, LANES), F32)
    fixed, planes, pairs = pl.pallas_call(
        import_kernel,
        out_shape=(blocks, operands, jax.ShapeDtypeStruct((2, TILES), jnp.int32)),
        in_specs=[HBM] * 5,
        out_specs=(VMEM, VMEM, VMEM),
        scratch_shapes=[pltpu.VMEM((CL, LANES), jnp.int32), pltpu.SMEM((16,), F32), dma(7), dma(5, 5), dma(5, 5)],
        compiler_params=params(0),
    )(*(held(v) for v in (type_radius, jnp.swapaxes(positions, 0, 1), charges, atom_types, tiles.T)))
    totals = tile_forces(pairs, tile_live, planes)
    places, planes, moving = pl.pallas_call(
        step_kernel,
        out_shape=(blocks, operands, shape((3, CL, LANES))),
        in_specs=[VMEM] * 3,
        out_specs=(VMEM, VMEM, VMEM),
        scratch_shapes=[partial, landing, dma(5, 3), dma(5, 3), dma(5, 3), dma(5, 3)],
        compiler_params=params(1),
    )(totals, fixed, jnp.swapaxes(velocities, 0, 1))
    totals = tile_forces(pairs, tile_live, planes)
    forces, arrived = pl.pallas_call(
        last_kernel,
        out_shape=(shape((3, CL, LANES)), shape((ARRIVING, 8, LANES))),
        in_specs=[VMEM] * 4,
        out_specs=(VMEM, VMEM),
        scratch_shapes=[
            partial,
            landing,
            pltpu.VMEM((ARRIVING, 8, LANES), F32),
            dma(5, 3),
            dma(5, 3),
            dma(TOWERS),
            dma(TOWERS),
            pltpu.SemaphoreType.DMA,
        ],
        compiler_params=params(2),
    )(totals, places, moving, destinations.T)
    return jnp.swapaxes(forces, 0, 1), arrived


def solution(mesh):
    home = ("gz", "gy", "gx")
    placed = (
        P(home, None, None),
        P(home, None, None),
        P(home, None),
        P(home, None),
        P(),
        P(home, None),
        P(home),
        P(home, None),
    )
    return jax.shard_map(
        local,
        mesh=mesh,
        in_specs=placed,
        out_specs=(P(home, None, None), P(home, None, None)),
        check_vma=False,
    )
```

```python
import functools

import jax
import jax.numpy as jnp
from jax import lax
from jax.experimental import pallas as pl
from jax.experimental.pallas import tpu as pltpu
from jax.sharding import PartitionSpec as P

coulomb = 0.3
time_step = 0.05

MESH = pl.DeviceIdType.MESH
F32 = jnp.float32
BF16 = jnp.bfloat16

CL = 64
LANES = 128
SLOTS = 6
ROWS = SLOTS * CL
CAPACITY = 4
TILES = 256
TOWERS = 32
ARRIVING = TOWERS * CAPACITY
UNROLL = 16
CENTER = 2.0
PLANES = 32
CHANNELS = 8
RADIUS, CHARGE = 3, 4


def split(x):
    high = x.astype(BF16).astype(F32)
    rest = x - high
    middle = rest.astype(BF16).astype(F32)
    return high, middle, rest - middle


def tile_kernel(listed, live, planes, totals, tiles, list_sem, store_a, store_b):
    listing = pltpu.make_async_copy(listed, tiles, list_sem)
    listing.start()
    line = lax.broadcasted_iota(jnp.int32, (8, LANES), 0)

    def clear(step, carry):
        for k in range(8):
            totals[pl.ds(pl.multiple_of(step * 64, 64) + k * 8, 8), :] = jnp.zeros((8, LANES), F32)
        return carry

    lax.fori_loop(0, ROWS // 8, clear, 0)
    listing.wait()

    sign = jnp.where(line % 4 == 3, 1.0, -1.0).astype(F32)
    live_count = live[0]

    def eight(plane, row):
        return planes[pl.ds(pl.multiple_of(row * 32, 32) + plane * 8, 8), :]

    blank = jnp.zeros((32, LANES), F32)

    def powers_of(group, pair, store):
        lefts, rights = [], []
        for v in range(2):
            a, b = tiles[0, group * UNROLL + 2 * pair + v], tiles[1, group * UNROLL + 2 * pair + v]
            near = eight(0, a) * sign
            lefts += [near, near, eight(1, a) * sign, eight(2, a)]
            r0, r1, r2 = eight(0, b), eight(1, b), eight(2, b)
            rights.append(
                jnp.concatenate([r0, pltpu.roll(r0, 4, 0), pltpu.roll(r1, 4, 0), pltpu.roll(r2, 4, 0)], axis=0)
            )
        left = jnp.concatenate(lefts, axis=0)
        right = jnp.concatenate(
            [jnp.concatenate([rights[0], blank], axis=1), jnp.concatenate([blank, rights[1]], axis=1)], axis=0
        )
        half_dist = lax.dot_general(
            left.astype(BF16), right.astype(BF16), (((0,), (0,)), ((), ())), preferred_element_type=F32
        )
        root = lax.rsqrt(half_dist)
        power = root * root * root
        high = power.astype(BF16)
        store[pair, 0:128, :] = high
        store[pair, 128:256, :] = (power - high.astype(F32)).astype(BF16)

    def sums_of(group, pair, store, sums):
        ids = [(tiles[0, group * UNROLL + 2 * pair + v], tiles[1, group * UNROLL + 2 * pair + v]) for v in range(2)]
        active = [jnp.where(group * UNROLL + 2 * pair + v < live_count, 1.0, 0.0).astype(F32) for v in range(2)]
        from_a = jnp.concatenate([eight(3, ids[v][0]) * active[v] for v in range(2)], axis=0).astype(BF16)
        from_b = jnp.concatenate([eight(3, ids[v][1]) * active[v] for v in range(2)], axis=0).astype(BF16)
        on_right = jnp.dot(jnp.concatenate([from_a, from_a], axis=1), store[pair], preferred_element_type=F32)
        across = jnp.concatenate(
            [
                jnp.concatenate([store[pair, 0:128, 0:128], store[pair, 128:256, 0:128]], axis=1),
                jnp.concatenate([store[pair, 0:128, 128:256], store[pair, 128:256, 128:256]], axis=1),
            ],
            axis=0,
        )
        on_left = lax.dot_general(
            jnp.concatenate([from_b, from_b], axis=1), across, (((1,), (1,)), ((), ())), preferred_element_type=F32
        )
        sums.append((ids[0][0], on_left[0:8, :LANES]))
        sums.append((ids[0][1], on_right[0:8, :LANES]))
        sums.append((ids[1][0], on_left[8:16, LANES:]))
        sums.append((ids[1][1], on_right[8:16, LANES:]))

    def add(sums):
        for row, value in sums:
            at = pl.ds(pl.multiple_of(row * 8, 8), 8)
            totals[at, :] = totals[at, :] + value

    half_group = UNROLL // 2
    for pair in range(half_group):
        powers_of(0, pair, store_a)

    def two_groups(step, carry):
        group = 2 * step
        for now, later, shift in ((store_a, store_b, 1), (store_b, store_a, 2)):
            sums = []
            for pair in range(half_group):
                sums_of(group + shift - 1, pair, now, sums)
                powers_of(jnp.minimum(group + shift, TILES // UNROLL - 1), pair, later)
            add(sums)
        return carry

    lax.fori_loop(0, (live_count + 2 * UNROLL - 1) // (2 * UNROLL), two_groups, 0)


def tile_forces(tiles, live, planes):
    return pl.pallas_call(
        tile_kernel,
        out_shape=jax.ShapeDtypeStruct((ROWS * 8, LANES), F32),
        in_specs=[
            pl.BlockSpec(memory_space=pltpu.VMEM),
            pl.BlockSpec(memory_space=pltpu.SMEM),
            pl.BlockSpec(memory_space=pltpu.VMEM),
        ],
        out_specs=pl.BlockSpec(memory_space=pltpu.VMEM),
        scratch_shapes=[
            pltpu.SMEM((2, TILES), jnp.int32),
            pltpu.SemaphoreType.DMA,
            pltpu.VMEM((UNROLL // 2, 256, 256), BF16),
            pltpu.VMEM((UNROLL // 2, 256, 256), BF16),
        ],
        compiler_params=pltpu.CompilerParams(vmem_limit_bytes=40 * 2**20),
        cost_estimate=pl.CostEstimate(flops=256 * 128 * 128 * 120, bytes_accessed=2 * 2**20, transcendentals=256 * 128 * 128),
    )(tiles, live, planes)


VMEM = pl.BlockSpec(memory_space=pltpu.VMEM)
HBM = pl.BlockSpec(memory_space=pltpu.HBM)
SMEM = pl.BlockSpec(memory_space=pltpu.SMEM)
BELOW, ABOVE = 4, 5


def here():
    return lax.axis_index("gz"), lax.axis_index("gy"), lax.axis_index("gx")


def neighbours():
    z, y, x = here()
    even = lax.rem(z, 2) == 0
    step = 1 - 2 * lax.rem(z, 2)
    pair = z + step
    return dict(
        core=(z, 1 - y, x),
        pair=(pair, y, x),
        cross=(pair, y, 1 - x),
        ahead=(lax.rem(z + 2 * step + TOWERS, TOWERS), y, x),
        behind=(lax.rem(z - 2 * step + TOWERS, TOWERS), y, x),
        mine=y * 2 + x,
        core_slot=(1 - y) * 2 + x,
        plate_slot=y * 2 + 1 - x,
        far_slot=(1 - y) * 2 + 1 - x,
        pair_slot=ABOVE - lax.rem(z, 2),
        other_slot=BELOW + lax.rem(z, 2),
    )


PARTNERS = ("core", "pair", "cross", "ahead", "behind")


def greet(devices):
    barrier = pltpu.get_barrier_semaphore()
    for device in devices:
        pl.semaphore_signal(barrier, inc=1, device_id=device, device_id_type=MESH)
    return barrier


def channel(slot, c):
    return pl.ds(pl.multiple_of(slot * (CHANNELS * CL) + c * CL, CL), CL)


def prepare(slot, blocks, planes):
    line = lax.broadcasted_iota(jnp.int32, (8, LANES), 0)
    upper = line < 4
    center = jnp.where(line < 3, CENTER, 0.0).astype(F32)

    def eight_clusters(step, carry):
        for k in range(8):
            first = pl.multiple_of(slot * (CHANNELS * CL) + step * 8, 8) + k
            to = pl.multiple_of(slot * (CL * PLANES) + step * (8 * PLANES), 8 * PLANES) + k * PLANES
            loaded = blocks[pl.ds(first, 8, stride=CL), :] - center
            twice = jnp.where(upper, loaded, pltpu.roll(loaded, 4, 0))
            charge = jnp.broadcast_to(loaded[4:5, :], (8, LANES))
            high, middle, low = split(twice)
            planes[pl.ds(to, 8), :] = jnp.where(upper, high, middle)
            planes[pl.ds(to + 8, 8), :] = jnp.where(upper, low, high)
            square = twice * twice
            square = square + pltpu.roll(square, 2, 0)
            square = 0.5 * (square + pltpu.roll(square, 1, 0))
            high, middle, low = split(square)
            parts = jnp.where(line == 0, high, jnp.where(line == 1, middle, low))
            planes[pl.ds(to + 16, 8), :] = jnp.where(line < 3, parts, jnp.where((line == 3) | (line == 7), 0.0, 1.0))
            weighted = jnp.where((line == 3) | (line == 7), 1.0, twice) * charge
            high = weighted.astype(BF16).astype(F32)
            planes[pl.ds(to + 24, 8), :] = jnp.where(upper, high, weighted - high)
        return carry

    lax.fori_loop(0, CL // 8, eight_clusters, 0)


def finish(slot, totals, blocks, partial):
    factor = coulomb * 0.5**1.5

    def eight_clusters(step, carry):
        rows = pl.ds(pl.multiple_of(step * 8, 8), 8)

        def plane(c):
            return blocks[pl.ds(pl.multiple_of(slot * (CHANNELS * CL) + c * CL + step * 8, 8), 8), :]

        def summed(k):
            first = pl.multiple_of(slot * (CL * 8) + step * 64, 64) + k
            return totals[pl.ds(first, 8, stride=8), :] + totals[pl.ds(first + 4, 8, stride=8), :]

        scale = factor * plane(CHARGE)
        whole = summed(3)
        for c in range(3):
            partial[slot, c, rows, :] = scale * ((plane(c) - CENTER) * whole - summed(c))
        return carry

    lax.fori_loop(0, CL // 8, eight_clusters, 0)


def clear_unused(blocks):
    for slot in range(SLOTS):
        for c in range(5, CHANNELS):
            blocks[channel(slot, c), :] = jnp.zeros((CL, LANES), F32)


def remote(source, target, send_sems, recv_sems, way, chunk, device):
    return pltpu.make_async_remote_copy(
        source, target, send_sems.at[way, chunk], recv_sems.at[way, chunk], device_id=device, device_id_type=MESH
    )


def spread(n, buffer, planes, channels, send_sems, recv_sems, ready):
    sent = []

    def send(way, chunk, slot, there, name):
        copy = remote(buffer.at[channel(slot, chunk)], buffer.at[channel(there, chunk)], send_sems, recv_sems, way, chunk, n[name])
        copy.start()
        sent.append(copy)

    def arrive(way, chunk, slot):
        place = buffer.at[channel(slot, chunk)]
        remote(place, place, send_sems, recv_sems, way, chunk, n["core"]).wait_recv()

    for c in channels:
        ready(c)
        send(1, c, n["mine"], n["other_slot"], "pair")
        send(0, c, n["mine"], n["mine"], "core")
    prepare(n["mine"], buffer, planes)
    for c in channels:
        arrive(1, c, n["pair_slot"])
        send(2, c, n["pair_slot"], n["mine"], "cross")
        send(3, c, n["pair_slot"], n["other_slot"], "ahead")
    prepare(n["pair_slot"], buffer, planes)
    for c in channels:
        arrive(0, c, n["core_slot"])
    prepare(n["core_slot"], buffer, planes)
    for c in channels:
        arrive(2, c, n["plate_slot"])
        send(4, c, n["plate_slot"], n["plate_slot"], "core")
    prepare(n["plate_slot"], buffer, planes)
    for c in channels:
        arrive(4, c, n["far_slot"])
    prepare(n["far_slot"], buffer, planes)
    for c in channels:
        arrive(3, c, n["other_slot"])
    prepare(n["other_slot"], buffer, planes)
    for copy in sent:
        copy.wait_send()


def gather_forces(n, totals, blocks, partial, landing, send_sems, recv_sems, meanwhile):
    sent = []

    def send(way, chunk, source, name):
        copy = remote(source, landing.at[way, chunk], send_sems, recv_sems, way, chunk, n[name])
        copy.start()
        sent.append(copy)

    def arrive(way, chunk):
        place = landing.at[way, chunk]
        remote(place, place, send_sems, recv_sems, way, chunk, n["core"]).wait_recv()

    for way, slot, name in ((0, "far_slot", "core"), (2, "other_slot", "behind"), (4, "core_slot", "core")):
        finish(n[slot], totals, blocks, partial)
        for c in range(3):
            send(way, c, partial.at[n[slot], c], name)
    for slot in ("plate_slot", "pair_slot", "mine"):
        finish(n[slot], totals, blocks, partial)
    meanwhile()
    for c in range(3):
        arrive(0, c)
        landing[5, c] = partial[n["plate_slot"], c] + landing[0, c]
        send(1, c, landing.at[5, c], "cross")
    for c in range(3):
        arrive(1, c)
        arrive(2, c)
        landing[6, c] = partial[n["pair_slot"], c] + landing[1, c] + landing[2, c]
        send(3, c, landing.at[6, c], "pair")

    def total(c):
        arrive(3, c)
        arrive(4, c)
        return partial[n["mine"], c] + landing[3, c] + landing[4, c]

    return total, sent


def import_kernel(radii, positions, charges, types, tiles, buffer, planes, pairs, kinds, table, load_sems, send_sems, recv_sems):
    n = neighbours()
    mine = n["mine"]
    loads = [pltpu.make_async_copy(positions.at[c], buffer.at[channel(mine, c)], load_sems.at[c]) for c in range(3)]
    loads.append(pltpu.make_async_copy(types, kinds, load_sems.at[3]))
    loads.append(pltpu.make_async_copy(charges, buffer.at[channel(mine, CHARGE)], load_sems.at[4]))
    loads.append(pltpu.make_async_copy(radii, table, load_sems.at[5]))
    loads.append(pltpu.make_async_copy(tiles, pairs, load_sems.at[6]))
    for load in loads:
        load.start()
    barrier = greet([n[name] for name in PARTNERS])
    clear_unused(buffer)
    pl.semaphore_wait(barrier, len(PARTNERS))

    def ready(c):
        loads[c].wait()
        if c == RADIUS:
            loads[5].wait()
            radius = jnp.zeros((CL, LANES), F32)
            for kind in range(16):
                radius = jnp.where(kinds[...] == kind, table[kind], radius)
            buffer[channel(mine, RADIUS), :] = radius
            loads[6].wait()

    spread(n, buffer, planes, (0, 1, 2, CHARGE, RADIUS), send_sems, recv_sems, ready)


def step_kernel(totals, fixed, velocities, places, planes, moving, partial, landing, send_sems, recv_sems, next_send, next_recv):
    n = neighbours()
    mine = n["mine"]
    barrier = greet([n[name] for name in PARTNERS])
    pl.semaphore_wait(barrier, len(PARTNERS))
    def meanwhile():
        for slot in range(SLOTS):
            for c in (RADIUS, CHARGE):
                places[channel(slot, c), :] = fixed[channel(slot, c), :]
        clear_unused(places)

    force, sent = gather_forces(n, totals, fixed, partial, landing, send_sems, recv_sems, meanwhile)

    def ready(c):
        speed = velocities[c] + time_step * force(c)
        moving[c] = speed
        places[channel(mine, c), :] = fixed[channel(mine, c), :] + time_step * speed

    spread(n, places, planes, range(3), next_send, next_recv, ready)
    for copy in sent:
        copy.wait_send()


def links(k):
    return min(k // 8, 4 - k // 8) + min(k // 2 % 4, 4 - k // 2 % 4) + k % 2


def last_kernel(
    totals, places, moving, destinations, forces_out, arrived, partial, landing, slots, send_sems, recv_sems, out_sems, in_sems, own_sem
):
    z, y, x = here()
    n = neighbours()
    mine = n["mine"]
    others = [(lax.rem(z + k, TOWERS), y, x) for k in range(1, TOWERS)]
    barrier = greet([n["core"], n["cross"]] + others)

    row = jnp.broadcast_to(destinations[...].astype(F32), (CL, CL))
    r = lax.broadcasted_iota(jnp.int32, (CL, CL), 0)
    c = lax.broadcasted_iota(jnp.int32, (CL, CL), 1)
    column = jnp.sum(jnp.where(r == c, row, 0.0), axis=1, keepdims=True)
    rank = jnp.sum(jnp.where((column == row) & (r < c), 1.0, 0.0), axis=0, keepdims=True)
    slot = row[0:1] * CAPACITY + rank
    select = (lax.broadcasted_iota(jnp.int32, (ARRIVING, CL), 0).astype(F32) == slot).astype(BF16)

    pl.semaphore_wait(barrier, 2 + TOWERS - 1)
    def keep(k, value):
        parts = split(value)
        slots[:, k, :] = sum(jnp.dot(select, part.astype(BF16), preferred_element_type=F32) for part in reversed(parts))

    def meanwhile():
        keep(6, places[channel(mine, CHARGE), :])
        keep(7, places[channel(mine, RADIUS), :])

    force, sent = gather_forces(n, totals, places, partial, landing, send_sems, recv_sems, meanwhile)
    for k in range(3):
        total = force(k)
        forces_out[k] = total
        speed = moving[k] + time_step * total
        keep(3 + k, speed)
        keep(k, places[channel(mine, k), :] + time_step * speed)

    def send(tower):
        return pltpu.make_async_remote_copy(
            slots.at[pl.ds(tower * CAPACITY, CAPACITY)],
            arrived.at[pl.ds(z * CAPACITY, CAPACITY)],
            out_sems.at[tower],
            in_sems.at[z],
            device_id=(tower, y, x),
            device_id_type=MESH,
        )

    def receive(tower):
        return pltpu.make_async_remote_copy(
            slots.at[pl.ds(tower * CAPACITY, CAPACITY)],
            arrived.at[pl.ds(tower * CAPACITY, CAPACITY)],
            out_sems.at[tower],
            in_sems.at[tower],
            device_id=(tower, y, x),
            device_id_type=MESH,
        )

    for k in sorted(range(1, TOWERS), key=links, reverse=True):
        send(lax.rem(z + k, TOWERS)).start()
    own = pltpu.make_async_copy(
        slots.at[pl.ds(z * CAPACITY, CAPACITY)], arrived.at[pl.ds(z * CAPACITY, CAPACITY)], own_sem
    )
    own.start()
    own.wait()
    for k in range(1, TOWERS):
        receive(lax.rem(z + TOWERS - k, TOWERS)).wait_recv()
    for k in range(1, TOWERS):
        send(lax.rem(z + k, TOWERS)).wait_send()
    for copy in sent:
        copy.wait_send()


def params(number):
    return pltpu.CompilerParams(collective_id=number, has_side_effects=True, vmem_limit_bytes=40 * 2**20)


def dma(*counts):
    return pltpu.SemaphoreType.DMA(counts)


def local(positions, velocities, charges, atom_types, type_radius, tiles, tile_live, destinations):
    held = functools.partial(pltpu.with_memory_space_constraint, memory_space=pltpu.HBM)
    shape = functools.partial(jax.ShapeDtypeStruct, dtype=F32)
    blocks = shape((SLOTS * CHANNELS * CL, LANES))
    operands = shape((ROWS * PLANES, LANES))
    partial = pltpu.VMEM((SLOTS, 3, CL, LANES), F32)
    landing = pltpu.VMEM((7, 3, CL, LANES), F32)
    fixed, planes, pairs = pl.pallas_call(
        import_kernel,
        out_shape=(blocks, operands, jax.ShapeDtypeStruct((2, TILES), jnp.int32)),
        in_specs=[HBM] * 5,
        out_specs=(VMEM, VMEM, VMEM),
        scratch_shapes=[pltpu.VMEM((CL, LANES), jnp.int32), pltpu.SMEM((16,), F32), dma(7), dma(5, 5), dma(5, 5)],
        compiler_params=params(0),
    )(*(held(v) for v in (type_radius, jnp.swapaxes(positions, 0, 1), charges, atom_types, tiles.T)))
    totals = tile_forces(pairs, tile_live, planes)
    places, planes, moving = pl.pallas_call(
        step_kernel,
        out_shape=(blocks, operands, shape((3, CL, LANES))),
        in_specs=[VMEM] * 3,
        out_specs=(VMEM, VMEM, VMEM),
        scratch_shapes=[partial, landing, dma(5, 3), dma(5, 3), dma(5, 3), dma(5, 3)],
        compiler_params=params(1),
    )(totals, fixed, jnp.swapaxes(velocities, 0, 1))
    totals = tile_forces(pairs, tile_live, planes)
    forces, arrived = pl.pallas_call(
        last_kernel,
        out_shape=(shape((3, CL, LANES)), shape((ARRIVING, 8, LANES))),
        in_specs=[VMEM] * 4,
        out_specs=(VMEM, VMEM),
        scratch_shapes=[
            partial,
            landing,
            pltpu.VMEM((ARRIVING, 8, LANES), F32),
            dma(5, 3),
            dma(5, 3),
            dma(TOWERS),
            dma(TOWERS),
            pltpu.SemaphoreType.DMA,
        ],
        compiler_params=params(2),
    )(totals, places, moving, destinations.T)
    return jnp.swapaxes(forces, 0, 1), arrived


def solution(mesh):
    home = ("gz", "gy", "gx")
    placed = (
        P(home, None, None),
        P(home, None, None),
        P(home, None),
        P(home, None),
        P(),
        P(home, None),
        P(home),
        P(home, None),
    )
    return jax.shard_map(
        local,
        mesh=mesh,
        in_specs=placed,
        out_specs=(P(home, None, None), P(home, None, None)),
        check_vma=False,
    )
```

```python
import functools

import jax
import jax.numpy as jnp
from jax import lax
from jax.experimental import pallas as pl
from jax.experimental.pallas import tpu as pltpu
from jax.sharding import PartitionSpec as P

coulomb = 0.3
time_step = 0.05

MESH = pl.DeviceIdType.MESH
F32 = jnp.float32
BF16 = jnp.bfloat16

CL = 64
LANES = 128
SLOTS = 6
ROWS = SLOTS * CL
CAPACITY = 4
TILES = 256
TOWERS = 32
ARRIVING = TOWERS * CAPACITY
UNROLL = 32
CENTER = 2.0
PLANES = 32
CHANNELS = 8
RADIUS, CHARGE = 3, 4


def split(x):
    high = x.astype(BF16).astype(F32)
    rest = x - high
    middle = rest.astype(BF16).astype(F32)
    return high, middle, rest - middle


def tile_kernel(listed, live, planes, totals, tiles, list_sem, store_a, store_b):
    listing = pltpu.make_async_copy(listed, tiles, list_sem)
    listing.start()
    line = lax.broadcasted_iota(jnp.int32, (8, LANES), 0)

    def clear(step, carry):
        for k in range(8):
            totals[pl.ds(pl.multiple_of(step * 64, 64) + k * 8, 8), :] = jnp.zeros((8, LANES), F32)
        return carry

    lax.fori_loop(0, ROWS // 8, clear, 0)
    listing.wait()

    sign = jnp.where(line % 4 == 3, 1.0, -1.0).astype(F32)
    live_count = live[0]

    def eight(plane, row):
        return planes[pl.ds(pl.multiple_of(row * 32, 32) + plane * 8, 8), :]

    blank = jnp.zeros((32, LANES), F32)

    def powers_of(group, pair, store):
        lefts, rights = [], []
        for v in range(2):
            a, b = tiles[0, group * UNROLL + 2 * pair + v], tiles[1, group * UNROLL + 2 * pair + v]
            near = eight(0, a) * sign
            lefts += [near, near, eight(1, a) * sign, eight(2, a)]
            r0, r1, r2 = eight(0, b), eight(1, b), eight(2, b)
            rights.append(
                jnp.concatenate([r0, pltpu.roll(r0, 4, 0), pltpu.roll(r1, 4, 0), pltpu.roll(r2, 4, 0)], axis=0)
            )
        left = jnp.concatenate(lefts, axis=0)
        right = jnp.concatenate(
            [jnp.concatenate([rights[0], blank], axis=1), jnp.concatenate([blank, rights[1]], axis=1)], axis=0
        )
        half_dist = lax.dot_general(
            left.astype(BF16), right.astype(BF16), (((0,), (0,)), ((), ())), preferred_element_type=F32
        )
        root = lax.rsqrt(half_dist)
        power = root * root * root
        high = power.astype(BF16)
        store[pair, 0:128, :] = high
        store[pair, 128:256, :] = (power - high.astype(F32)).astype(BF16)

    def sums_of(group, pair, store, sums):
        ids = [(tiles[0, group * UNROLL + 2 * pair + v], tiles[1, group * UNROLL + 2 * pair + v]) for v in range(2)]
        active = [jnp.where(group * UNROLL + 2 * pair + v < live_count, 1.0, 0.0).astype(F32) for v in range(2)]
        from_a = jnp.concatenate([eight(3, ids[v][0]) * active[v] for v in range(2)], axis=0).astype(BF16)
        from_b = jnp.concatenate([eight(3, ids[v][1]) * active[v] for v in range(2)], axis=0).astype(BF16)
        on_right = jnp.dot(jnp.concatenate([from_a, from_a], axis=1), store[pair], preferred_element_type=F32)
        across = jnp.concatenate(
            [
                jnp.concatenate([store[pair, 0:128, 0:128], store[pair, 128:256, 0:128]], axis=1),
                jnp.concatenate([store[pair, 0:128, 128:256], store[pair, 128:256, 128:256]], axis=1),
            ],
            axis=0,
        )
        on_left = lax.dot_general(
            jnp.concatenate([from_b, from_b], axis=1), across, (((1,), (1,)), ((), ())), preferred_element_type=F32
        )
        sums.append((ids[0][0], on_left[0:8, :LANES]))
        sums.append((ids[0][1], on_right[0:8, :LANES]))
        sums.append((ids[1][0], on_left[8:16, LANES:]))
        sums.append((ids[1][1], on_right[8:16, LANES:]))

    def add(sums):
        for row, value in sums:
            at = pl.ds(pl.multiple_of(row * 8, 8), 8)
            totals[at, :] = totals[at, :] + value

    half_group = UNROLL // 2
    for pair in range(half_group):
        powers_of(0, pair, store_a)

    def two_groups(step, carry):
        group = 2 * step
        for now, later, shift in ((store_a, store_b, 1), (store_b, store_a, 2)):
            sums = []
            for pair in range(half_group):
                sums_of(group + shift - 1, pair, now, sums)
                powers_of(jnp.minimum(group + shift, TILES // UNROLL - 1), pair, later)
            add(sums)
        return carry

    lax.fori_loop(0, (live_count + 2 * UNROLL - 1) // (2 * UNROLL), two_groups, 0)


def tile_forces(tiles, live, planes):
    return pl.pallas_call(
        tile_kernel,
        out_shape=jax.ShapeDtypeStruct((ROWS * 8, LANES), F32),
        in_specs=[
            pl.BlockSpec(memory_space=pltpu.VMEM),
            pl.BlockSpec(memory_space=pltpu.SMEM),
            pl.BlockSpec(memory_space=pltpu.VMEM),
        ],
        out_specs=pl.BlockSpec(memory_space=pltpu.VMEM),
        scratch_shapes=[
            pltpu.SMEM((2, TILES), jnp.int32),
            pltpu.SemaphoreType.DMA,
            pltpu.VMEM((UNROLL // 2, 256, 256), BF16),
            pltpu.VMEM((UNROLL // 2, 256, 256), BF16),
        ],
        compiler_params=pltpu.CompilerParams(vmem_limit_bytes=40 * 2**20),
        cost_estimate=pl.CostEstimate(flops=256 * 128 * 128 * 120, bytes_accessed=2 * 2**20, transcendentals=256 * 128 * 128),
    )(tiles, live, planes)


VMEM = pl.BlockSpec(memory_space=pltpu.VMEM)
HBM = pl.BlockSpec(memory_space=pltpu.HBM)
SMEM = pl.BlockSpec(memory_space=pltpu.SMEM)
BELOW, ABOVE = 4, 5


def here():
    return lax.axis_index("gz"), lax.axis_index("gy"), lax.axis_index("gx")


def neighbours():
    z, y, x = here()
    even = lax.rem(z, 2) == 0
    step = 1 - 2 * lax.rem(z, 2)
    pair = z + step
    return dict(
        core=(z, 1 - y, x),
        pair=(pair, y, x),
        cross=(pair, y, 1 - x),
        ahead=(lax.rem(z + 2 * step + TOWERS, TOWERS), y, x),
        behind=(lax.rem(z - 2 * step + TOWERS, TOWERS), y, x),
        mine=y * 2 + x,
        core_slot=(1 - y) * 2 + x,
        plate_slot=y * 2 + 1 - x,
        far_slot=(1 - y) * 2 + 1 - x,
        pair_slot=ABOVE - lax.rem(z, 2),
        other_slot=BELOW + lax.rem(z, 2),
    )


PARTNERS = ("core", "pair", "cross", "ahead", "behind")


def greet(devices):
    barrier = pltpu.get_barrier_semaphore()
    for device in devices:
        pl.semaphore_signal(barrier, inc=1, device_id=device, device_id_type=MESH)
    return barrier


def channel(slot, c):
    return pl.ds(pl.multiple_of(slot * (CHANNELS * CL) + c * CL, CL), CL)


def prepare(slot, blocks, planes):
    line = lax.broadcasted_iota(jnp.int32, (8, LANES), 0)
    upper = line < 4
    center = jnp.where(line < 3, CENTER, 0.0).astype(F32)

    def eight_clusters(step, carry):
        for k in range(8):
            first = pl.multiple_of(slot * (CHANNELS * CL) + step * 8, 8) + k
            to = pl.multiple_of(slot * (CL * PLANES) + step * (8 * PLANES), 8 * PLANES) + k * PLANES
            loaded = blocks[pl.ds(first, 8, stride=CL), :] - center
            twice = jnp.where(upper, loaded, pltpu.roll(loaded, 4, 0))
            charge = jnp.broadcast_to(loaded[4:5, :], (8, LANES))
            high, middle, low = split(twice)
            planes[pl.ds(to, 8), :] = jnp.where(upper, high, middle)
            planes[pl.ds(to + 8, 8), :] = jnp.where(upper, low, high)
            square = twice * twice
            square = square + pltpu.roll(square, 2, 0)
            square = 0.5 * (square + pltpu.roll(square, 1, 0))
            high, middle, low = split(square)
            parts = jnp.where(line == 0, high, jnp.where(line == 1, middle, low))
            planes[pl.ds(to + 16, 8), :] = jnp.where(line < 3, parts, jnp.where((line == 3) | (line == 7), 0.0, 1.0))
            weighted = jnp.where((line == 3) | (line == 7), 1.0, twice) * charge
            high = weighted.astype(BF16).astype(F32)
            planes[pl.ds(to + 24, 8), :] = jnp.where(upper, high, weighted - high)
        return carry

    lax.fori_loop(0, CL // 8, eight_clusters, 0)


def finish(slot, totals, blocks, partial):
    factor = coulomb * 0.5**1.5

    def eight_clusters(step, carry):
        rows = pl.ds(pl.multiple_of(step * 8, 8), 8)

        def plane(c):
            return blocks[pl.ds(pl.multiple_of(slot * (CHANNELS * CL) + c * CL + step * 8, 8), 8), :]

        def summed(k):
            first = pl.multiple_of(slot * (CL * 8) + step * 64, 64) + k
            return totals[pl.ds(first, 8, stride=8), :] + totals[pl.ds(first + 4, 8, stride=8), :]

        scale = factor * plane(CHARGE)
        whole = summed(3)
        for c in range(3):
            partial[slot, c, rows, :] = scale * ((plane(c) - CENTER) * whole - summed(c))
        return carry

    lax.fori_loop(0, CL // 8, eight_clusters, 0)


def clear_unused(blocks):
    for slot in range(SLOTS):
        for c in range(5, CHANNELS):
            blocks[channel(slot, c), :] = jnp.zeros((CL, LANES), F32)


def remote(source, target, send_sems, recv_sems, way, chunk, device):
    return pltpu.make_async_remote_copy(
        source, target, send_sems.at[way, chunk], recv_sems.at[way, chunk], device_id=device, device_id_type=MESH
    )


def spread(n, buffer, planes, channels, send_sems, recv_sems, ready):
    sent = []

    def send(way, chunk, slot, there, name):
        copy = remote(buffer.at[channel(slot, chunk)], buffer.at[channel(there, chunk)], send_sems, recv_sems, way, chunk, n[name])
        copy.start()
        sent.append(copy)

    def arrive(way, chunk, slot):
        place = buffer.at[channel(slot, chunk)]
        remote(place, place, send_sems, recv_sems, way, chunk, n["core"]).wait_recv()

    for c in channels:
        ready(c)
        send(1, c, n["mine"], n["other_slot"], "pair")
        send(0, c, n["mine"], n["mine"], "core")
    prepare(n["mine"], buffer, planes)
    for c in channels:
        arrive(1, c, n["pair_slot"])
        send(2, c, n["pair_slot"], n["mine"], "cross")
        send(3, c, n["pair_slot"], n["other_slot"], "ahead")
    prepare(n["pair_slot"], buffer, planes)
    for c in channels:
        arrive(0, c, n["core_slot"])
    prepare(n["core_slot"], buffer, planes)
    for c in channels:
        arrive(2, c, n["plate_slot"])
        send(4, c, n["plate_slot"], n["plate_slot"], "core")
    prepare(n["plate_slot"], buffer, planes)
    for c in channels:
        arrive(4, c, n["far_slot"])
    prepare(n["far_slot"], buffer, planes)
    for c in channels:
        arrive(3, c, n["other_slot"])
    prepare(n["other_slot"], buffer, planes)
    for copy in sent:
        copy.wait_send()


def gather_forces(n, totals, blocks, partial, landing, send_sems, recv_sems, meanwhile):
    sent = []

    def send(way, chunk, source, name):
        copy = remote(source, landing.at[way, chunk], send_sems, recv_sems, way, chunk, n[name])
        copy.start()
        sent.append(copy)

    def arrive(way, chunk):
        place = landing.at[way, chunk]
        remote(place, place, send_sems, recv_sems, way, chunk, n["core"]).wait_recv()

    for way, slot, name in ((0, "far_slot", "core"), (2, "other_slot", "behind"), (4, "core_slot", "core")):
        finish(n[slot], totals, blocks, partial)
        for c in range(3):
            send(way, c, partial.at[n[slot], c], name)
    for slot in ("plate_slot", "pair_slot", "mine"):
        finish(n[slot], totals, blocks, partial)
    meanwhile()
    for c in range(3):
        arrive(0, c)
        landing[5, c] = partial[n["plate_slot"], c] + landing[0, c]
        send(1, c, landing.at[5, c], "cross")
    for c in range(3):
        arrive(1, c)
        arrive(2, c)
        landing[6, c] = partial[n["pair_slot"], c] + landing[1, c] + landing[2, c]
        send(3, c, landing.at[6, c], "pair")

    def total(c):
        arrive(3, c)
        arrive(4, c)
        return partial[n["mine"], c] + landing[3, c] + landing[4, c]

    return total, sent


def import_kernel(radii, positions, charges, types, tiles, buffer, planes, pairs, kinds, table, load_sems, send_sems, recv_sems):
    n = neighbours()
    mine = n["mine"]
    loads = [pltpu.make_async_copy(positions.at[c], buffer.at[channel(mine, c)], load_sems.at[c]) for c in range(3)]
    loads.append(pltpu.make_async_copy(types, kinds, load_sems.at[3]))
    loads.append(pltpu.make_async_copy(charges, buffer.at[channel(mine, CHARGE)], load_sems.at[4]))
    loads.append(pltpu.make_async_copy(radii, table, load_sems.at[5]))
    loads.append(pltpu.make_async_copy(tiles, pairs, load_sems.at[6]))
    for load in loads:
        load.start()
    barrier = greet([n[name] for name in PARTNERS])
    clear_unused(buffer)
    pl.semaphore_wait(barrier, len(PARTNERS))

    def ready(c):
        loads[c].wait()
        if c == RADIUS:
            loads[5].wait()
            radius = jnp.zeros((CL, LANES), F32)
            for kind in range(16):
                radius = jnp.where(kinds[...] == kind, table[kind], radius)
            buffer[channel(mine, RADIUS), :] = radius
            loads[6].wait()

    spread(n, buffer, planes, (0, 1, 2, CHARGE, RADIUS), send_sems, recv_sems, ready)


def step_kernel(totals, fixed, velocities, places, planes, moving, partial, landing, send_sems, recv_sems, next_send, next_recv):
    n = neighbours()
    mine = n["mine"]
    barrier = greet([n[name] for name in PARTNERS])
    pl.semaphore_wait(barrier, len(PARTNERS))
    def meanwhile():
        for slot in range(SLOTS):
            for c in (RADIUS, CHARGE):
                places[channel(slot, c), :] = fixed[channel(slot, c), :]
        clear_unused(places)

    force, sent = gather_forces(n, totals, fixed, partial, landing, send_sems, recv_sems, meanwhile)

    def ready(c):
        speed = velocities[c] + time_step * force(c)
        moving[c] = speed
        places[channel(mine, c), :] = fixed[channel(mine, c), :] + time_step * speed

    spread(n, places, planes, range(3), next_send, next_recv, ready)
    for copy in sent:
        copy.wait_send()


def links(k):
    return min(k // 8, 4 - k // 8) + min(k // 2 % 4, 4 - k // 2 % 4) + k % 2


def last_kernel(
    totals, places, moving, destinations, forces_out, arrived, partial, landing, slots, send_sems, recv_sems, out_sems, in_sems, own_sem
):
    z, y, x = here()
    n = neighbours()
    mine = n["mine"]
    others = [(lax.rem(z + k, TOWERS), y, x) for k in range(1, TOWERS)]
    barrier = greet([n["core"], n["cross"]] + others)

    row = jnp.broadcast_to(destinations[...].astype(F32), (CL, CL))
    r = lax.broadcasted_iota(jnp.int32, (CL, CL), 0)
    c = lax.broadcasted_iota(jnp.int32, (CL, CL), 1)
    column = jnp.sum(jnp.where(r == c, row, 0.0), axis=1, keepdims=True)
    rank = jnp.sum(jnp.where((column == row) & (r < c), 1.0, 0.0), axis=0, keepdims=True)
    slot = row[0:1] * CAPACITY + rank
    select = (lax.broadcasted_iota(jnp.int32, (ARRIVING, CL), 0).astype(F32) == slot).astype(BF16)

    pl.semaphore_wait(barrier, 2 + TOWERS - 1)
    def keep(k, value):
        parts = split(value)
        slots[:, k, :] = sum(jnp.dot(select, part.astype(BF16), preferred_element_type=F32) for part in reversed(parts))

    def meanwhile():
        keep(6, places[channel(mine, CHARGE), :])
        keep(7, places[channel(mine, RADIUS), :])

    force, sent = gather_forces(n, totals, places, partial, landing, send_sems, recv_sems, meanwhile)
    for k in range(3):
        total = force(k)
        forces_out[k] = total
        speed = moving[k] + time_step * total
        keep(3 + k, speed)
        keep(k, places[channel(mine, k), :] + time_step * speed)

    def send(tower):
        return pltpu.make_async_remote_copy(
            slots.at[pl.ds(tower * CAPACITY, CAPACITY)],
            arrived.at[pl.ds(z * CAPACITY, CAPACITY)],
            out_sems.at[tower],
            in_sems.at[z],
            device_id=(tower, y, x),
            device_id_type=MESH,
        )

    def receive(tower):
        return pltpu.make_async_remote_copy(
            slots.at[pl.ds(tower * CAPACITY, CAPACITY)],
            arrived.at[pl.ds(tower * CAPACITY, CAPACITY)],
            out_sems.at[tower],
            in_sems.at[tower],
            device_id=(tower, y, x),
            device_id_type=MESH,
        )

    for k in sorted(range(1, TOWERS), key=links, reverse=True):
        send(lax.rem(z + k, TOWERS)).start()
    own = pltpu.make_async_copy(
        slots.at[pl.ds(z * CAPACITY, CAPACITY)], arrived.at[pl.ds(z * CAPACITY, CAPACITY)], own_sem
    )
    own.start()
    own.wait()
    for k in range(1, TOWERS):
        receive(lax.rem(z + TOWERS - k, TOWERS)).wait_recv()
    for k in range(1, TOWERS):
        send(lax.rem(z + k, TOWERS)).wait_send()
    for copy in sent:
        copy.wait_send()


def params(number):
    return pltpu.CompilerParams(collective_id=number, has_side_effects=True, vmem_limit_bytes=40 * 2**20)


def dma(*counts):
    return pltpu.SemaphoreType.DMA(counts)


def local(positions, velocities, charges, atom_types, type_radius, tiles, tile_live, destinations):
    held = functools.partial(pltpu.with_memory_space_constraint, memory_space=pltpu.HBM)
    shape = functools.partial(jax.ShapeDtypeStruct, dtype=F32)
    blocks = shape((SLOTS * CHANNELS * CL, LANES))
    operands = shape((ROWS * PLANES, LANES))
    partial = pltpu.VMEM((SLOTS, 3, CL, LANES), F32)
    landing = pltpu.VMEM((7, 3, CL, LANES), F32)
    fixed, planes, pairs = pl.pallas_call(
        import_kernel,
        out_shape=(blocks, operands, jax.ShapeDtypeStruct((2, TILES), jnp.int32)),
        in_specs=[HBM] * 5,
        out_specs=(VMEM, VMEM, VMEM),
        scratch_shapes=[pltpu.VMEM((CL, LANES), jnp.int32), pltpu.SMEM((16,), F32), dma(7), dma(5, 5), dma(5, 5)],
        compiler_params=params(0),
    )(*(held(v) for v in (type_radius, jnp.swapaxes(positions, 0, 1), charges, atom_types, tiles.T)))
    totals = tile_forces(pairs, tile_live, planes)
    places, planes, moving = pl.pallas_call(
        step_kernel,
        out_shape=(blocks, operands, shape((3, CL, LANES))),
        in_specs=[VMEM] * 3,
        out_specs=(VMEM, VMEM, VMEM),
        scratch_shapes=[partial, landing, dma(5, 3), dma(5, 3), dma(5, 3), dma(5, 3)],
        compiler_params=params(1),
    )(totals, fixed, jnp.swapaxes(velocities, 0, 1))
    totals = tile_forces(pairs, tile_live, planes)
    forces, arrived = pl.pallas_call(
        last_kernel,
        out_shape=(shape((3, CL, LANES)), shape((ARRIVING, 8, LANES))),
        in_specs=[VMEM] * 4,
        out_specs=(VMEM, VMEM),
        scratch_shapes=[
            partial,
            landing,
            pltpu.VMEM((ARRIVING, 8, LANES), F32),
            dma(5, 3),
            dma(5, 3),
            dma(TOWERS),
            dma(TOWERS),
            pltpu.SemaphoreType.DMA,
        ],
        compiler_params=params(2),
    )(totals, places, moving, destinations.T)
    return jnp.swapaxes(forces, 0, 1), arrived


def solution(mesh):
    home = ("gz", "gy", "gx")
    placed = (
        P(home, None, None),
        P(home, None, None),
        P(home, None),
        P(home, None),
        P(),
        P(home, None),
        P(home),
        P(home, None),
    )
    return jax.shard_map(
        local,
        mesh=mesh,
        in_specs=placed,
        out_specs=(P(home, None, None), P(home, None, None)),
        check_vma=False,
    )
```

```python
import functools

import jax
import jax.numpy as jnp
from jax import lax
from jax.experimental import pallas as pl
from jax.experimental.pallas import tpu as pltpu
from jax.sharding import PartitionSpec as P

coulomb = 0.3
time_step = 0.05

MESH = pl.DeviceIdType.MESH
F32 = jnp.float32
BF16 = jnp.bfloat16

CL = 64
LANES = 128
SLOTS = 6
ROWS = SLOTS * CL
CAPACITY = 4
TILES = 256
TOWERS = 32
ARRIVING = TOWERS * CAPACITY
UNROLL = 32
CENTER = 2.0
PLANES = 32
CHANNELS = 8
RADIUS, CHARGE = 3, 4


def split(x):
    high = x.astype(BF16).astype(F32)
    rest = x - high
    middle = rest.astype(BF16).astype(F32)
    return high, middle, rest - middle


def tile_kernel(listed, live, planes, totals, tiles, list_sem, store_a, store_b):
    listing = pltpu.make_async_copy(listed, tiles, list_sem)
    listing.start()
    line = lax.broadcasted_iota(jnp.int32, (8, LANES), 0)

    def clear(step, carry):
        for k in range(8):
            totals[pl.ds(pl.multiple_of(step * 64, 64) + k * 8, 8), :] = jnp.zeros((8, LANES), F32)
        return carry

    lax.fori_loop(0, ROWS // 8, clear, 0)
    listing.wait()

    sign = jnp.where(line % 4 == 3, 1.0, -1.0).astype(F32)
    live_count = live[0]

    def eight(plane, row):
        return planes[pl.ds(pl.multiple_of(row * 32, 32) + plane * 8, 8), :]

    blank = jnp.zeros((32, LANES), F32)

    def powers_of(group, pair, store):
        lefts, rights = [], []
        for v in range(2):
            a, b = tiles[0, group * UNROLL + 2 * pair + v], tiles[1, group * UNROLL + 2 * pair + v]
            near = eight(0, a) * sign
            lefts += [near, near, eight(1, a) * sign, eight(2, a)]
            r0, r1, r2 = eight(0, b), eight(1, b), eight(2, b)
            rights.append(
                jnp.concatenate([r0, pltpu.roll(r0, 4, 0), pltpu.roll(r1, 4, 0), pltpu.roll(r2, 4, 0)], axis=0)
            )
        left = jnp.concatenate(lefts, axis=0)
        right = jnp.concatenate(
            [jnp.concatenate([rights[0], blank], axis=1), jnp.concatenate([blank, rights[1]], axis=1)], axis=0
        )
        half_dist = lax.dot_general(
            left.astype(BF16), right.astype(BF16), (((0,), (0,)), ((), ())), preferred_element_type=F32
        )
        root = lax.rsqrt(half_dist)
        power = root * root * root
        high = power.astype(BF16)
        store[pair, 0:128, :] = high
        store[pair, 128:256, :] = (power - high.astype(F32)).astype(BF16)

    def sums_of(group, pair, store, sums):
        ids = [(tiles[0, group * UNROLL + 2 * pair + v], tiles[1, group * UNROLL + 2 * pair + v]) for v in range(2)]
        active = [jnp.where(group * UNROLL + 2 * pair + v < live_count, 1.0, 0.0).astype(F32) for v in range(2)]
        from_a = jnp.concatenate([eight(3, ids[v][0]) * active[v] for v in range(2)], axis=0).astype(BF16)
        from_b = jnp.concatenate([eight(3, ids[v][1]) * active[v] for v in range(2)], axis=0).astype(BF16)
        on_right = jnp.dot(jnp.concatenate([from_a, from_a], axis=1), store[pair], preferred_element_type=F32)
        across = jnp.concatenate(
            [
                jnp.concatenate([store[pair, 0:128, 0:128], store[pair, 128:256, 0:128]], axis=1),
                jnp.concatenate([store[pair, 0:128, 128:256], store[pair, 128:256, 128:256]], axis=1),
            ],
            axis=0,
        )
        on_left = lax.dot_general(
            jnp.concatenate([from_b, from_b], axis=1), across, (((1,), (1,)), ((), ())), preferred_element_type=F32
        )
        sums.append((ids[0][0], on_left[0:8, :LANES]))
        sums.append((ids[0][1], on_right[0:8, :LANES]))
        sums.append((ids[1][0], on_left[8:16, LANES:]))
        sums.append((ids[1][1], on_right[8:16, LANES:]))

    def add(sums):
        for row, value in sums:
            at = pl.ds(pl.multiple_of(row * 8, 8), 8)
            totals[at, :] = totals[at, :] + value

    half_group = UNROLL // 2
    for pair in range(half_group):
        powers_of(0, pair, store_a)

    def two_groups(step, carry):
        group = 2 * step
        for now, later, shift in ((store_a, store_b, 1), (store_b, store_a, 2)):
            sums = []
            for pair in range(half_group):
                sums_of(group + shift - 1, pair, now, sums)
                powers_of(jnp.minimum(group + shift, TILES // UNROLL - 1), pair, later)
            add(sums)
        return carry

    lax.fori_loop(0, (live_count + 2 * UNROLL - 1) // (2 * UNROLL), two_groups, 0)


def tile_forces(tiles, live, planes):
    return pl.pallas_call(
        tile_kernel,
        out_shape=jax.ShapeDtypeStruct((ROWS * 8, LANES), F32),
        in_specs=[
            pl.BlockSpec(memory_space=pltpu.VMEM),
            pl.BlockSpec(memory_space=pltpu.SMEM),
            pl.BlockSpec(memory_space=pltpu.VMEM),
        ],
        out_specs=pl.BlockSpec(memory_space=pltpu.VMEM),
        scratch_shapes=[
            pltpu.SMEM((2, TILES), jnp.int32),
            pltpu.SemaphoreType.DMA,
            pltpu.VMEM((UNROLL // 2, 256, 256), BF16),
            pltpu.VMEM((UNROLL // 2, 256, 256), BF16),
        ],
        compiler_params=pltpu.CompilerParams(vmem_limit_bytes=40 * 2**20),
        cost_estimate=pl.CostEstimate(flops=256 * 128 * 128 * 120, bytes_accessed=2 * 2**20, transcendentals=256 * 128 * 128),
    )(tiles, live, planes)


VMEM = pl.BlockSpec(memory_space=pltpu.VMEM)
HBM = pl.BlockSpec(memory_space=pltpu.HBM)
SMEM = pl.BlockSpec(memory_space=pltpu.SMEM)
BELOW, ABOVE = 4, 5


def here():
    return lax.axis_index("gz"), lax.axis_index("gy"), lax.axis_index("gx")


def neighbours():
    z, y, x = here()
    even = lax.rem(z, 2) == 0
    step = 1 - 2 * lax.rem(z, 2)
    pair = z + step
    return dict(
        core=(z, 1 - y, x),
        pair=(pair, y, x),
        cross=(pair, y, 1 - x),
        ahead=(lax.rem(z + 2 * step + TOWERS, TOWERS), y, x),
        behind=(lax.rem(z - 2 * step + TOWERS, TOWERS), y, x),
        mine=y * 2 + x,
        core_slot=(1 - y) * 2 + x,
        plate_slot=y * 2 + 1 - x,
        far_slot=(1 - y) * 2 + 1 - x,
        pair_slot=ABOVE - lax.rem(z, 2),
        other_slot=BELOW + lax.rem(z, 2),
    )


PARTNERS = ("core", "pair", "cross", "ahead", "behind")


def greet(devices):
    barrier = pltpu.get_barrier_semaphore()
    for device in devices:
        pl.semaphore_signal(barrier, inc=1, device_id=device, device_id_type=MESH)
    return barrier


def channel(slot, c):
    return pl.ds(pl.multiple_of(slot * (CHANNELS * CL) + c * CL, CL), CL)


def prepare(slot, blocks, planes):
    line = lax.broadcasted_iota(jnp.int32, (8, LANES), 0)
    upper = line < 4
    center = jnp.where(line < 3, CENTER, 0.0).astype(F32)

    def eight_clusters(step, carry):
        for k in range(8):
            first = pl.multiple_of(slot * (CHANNELS * CL) + step * 8, 8) + k
            to = pl.multiple_of(slot * (CL * PLANES) + step * (8 * PLANES), 8 * PLANES) + k * PLANES
            loaded = blocks[pl.ds(first, 8, stride=CL), :] - center
            twice = jnp.where(upper, loaded, pltpu.roll(loaded, 4, 0))
            charge = jnp.broadcast_to(loaded[4:5, :], (8, LANES))
            high, middle, low = split(twice)
            planes[pl.ds(to, 8), :] = jnp.where(upper, high, middle)
            planes[pl.ds(to + 8, 8), :] = jnp.where(upper, low, high)
            square = twice * twice
            square = square + pltpu.roll(square, 2, 0)
            square = 0.5 * (square + pltpu.roll(square, 1, 0))
            high, middle, low = split(square)
            parts = jnp.where(line == 0, high, jnp.where(line == 1, middle, low))
            planes[pl.ds(to + 16, 8), :] = jnp.where(line < 3, parts, jnp.where((line == 3) | (line == 7), 0.0, 1.0))
            weighted = jnp.where((line == 3) | (line == 7), 1.0, twice) * charge
            high = weighted.astype(BF16).astype(F32)
            planes[pl.ds(to + 24, 8), :] = jnp.where(upper, high, weighted - high)
        return carry

    lax.fori_loop(0, CL // 8, eight_clusters, 0)


def finish(slot, totals, blocks, partial):
    factor = coulomb * 0.5**1.5

    def eight_clusters(step, carry):
        rows = pl.ds(pl.multiple_of(step * 8, 8), 8)

        def plane(c):
            return blocks[pl.ds(pl.multiple_of(slot * (CHANNELS * CL) + c * CL + step * 8, 8), 8), :]

        def summed(k):
            first = pl.multiple_of(slot * (CL * 8) + step * 64, 64) + k
            return totals[pl.ds(first, 8, stride=8), :] + totals[pl.ds(first + 4, 8, stride=8), :]

        scale = factor * plane(CHARGE)
        whole = summed(3)
        for c in range(3):
            partial[slot, c, rows, :] = scale * ((plane(c) - CENTER) * whole - summed(c))
        return carry

    lax.fori_loop(0, CL // 8, eight_clusters, 0)


def clear_unused(blocks):
    for slot in range(SLOTS):
        for c in range(5, CHANNELS):
            blocks[channel(slot, c), :] = jnp.zeros((CL, LANES), F32)


def remote(source, target, send_sems, recv_sems, way, chunk, device):
    return pltpu.make_async_remote_copy(
        source, target, send_sems.at[way, chunk], recv_sems.at[way, chunk], device_id=device, device_id_type=MESH
    )


def spread(n, buffer, planes, channels, send_sems, recv_sems, ready):
    sent = []

    def send(way, chunk, slot, there, name):
        copy = remote(buffer.at[channel(slot, chunk)], buffer.at[channel(there, chunk)], send_sems, recv_sems, way, chunk, n[name])
        copy.start()
        sent.append(copy)

    def arrive(way, chunk, slot):
        place = buffer.at[channel(slot, chunk)]
        remote(place, place, send_sems, recv_sems, way, chunk, n["core"]).wait_recv()

    for c in channels:
        ready(c)
        send(1, c, n["mine"], n["other_slot"], "pair")
        send(0, c, n["mine"], n["mine"], "core")
    prepare(n["mine"], buffer, planes)
    for c in channels:
        arrive(1, c, n["pair_slot"])
        send(2, c, n["pair_slot"], n["mine"], "cross")
        send(3, c, n["pair_slot"], n["other_slot"], "ahead")
    prepare(n["pair_slot"], buffer, planes)
    for c in channels:
        arrive(0, c, n["core_slot"])
    prepare(n["core_slot"], buffer, planes)
    for c in channels:
        arrive(2, c, n["plate_slot"])
        send(4, c, n["plate_slot"], n["plate_slot"], "core")
    prepare(n["plate_slot"], buffer, planes)
    for c in channels:
        arrive(4, c, n["far_slot"])
    prepare(n["far_slot"], buffer, planes)
    for c in channels:
        arrive(3, c, n["other_slot"])
    prepare(n["other_slot"], buffer, planes)
    for copy in sent:
        copy.wait_send()


def gather_forces(n, totals, blocks, partial, landing, send_sems, recv_sems, meanwhile):
    sent = []

    def send(way, chunk, source, name):
        copy = remote(source, landing.at[way, chunk], send_sems, recv_sems, way, chunk, n[name])
        copy.start()
        sent.append(copy)

    def arrive(way, chunk):
        place = landing.at[way, chunk]
        remote(place, place, send_sems, recv_sems, way, chunk, n["core"]).wait_recv()

    for way, slot, name in ((2, "other_slot", "behind"), (0, "far_slot", "core"), (4, "core_slot", "core")):
        finish(n[slot], totals, blocks, partial)
        for c in range(3):
            send(way, c, partial.at[n[slot], c], name)
    for slot in ("plate_slot", "pair_slot", "mine"):
        finish(n[slot], totals, blocks, partial)
    meanwhile()
    for c in range(3):
        arrive(0, c)
        landing[5, c] = partial[n["plate_slot"], c] + landing[0, c]
        send(1, c, landing.at[5, c], "cross")
    for c in range(3):
        arrive(1, c)
        arrive(2, c)
        landing[6, c] = partial[n["pair_slot"], c] + landing[1, c] + landing[2, c]
        send(3, c, landing.at[6, c], "pair")

    def total(c):
        arrive(3, c)
        arrive(4, c)
        return partial[n["mine"], c] + landing[3, c] + landing[4, c]

    return total, sent


def import_kernel(radii, positions, charges, types, tiles, buffer, planes, pairs, kinds, table, load_sems, send_sems, recv_sems):
    n = neighbours()
    mine = n["mine"]
    loads = [pltpu.make_async_copy(positions.at[c], buffer.at[channel(mine, c)], load_sems.at[c]) for c in range(3)]
    loads.append(pltpu.make_async_copy(types, kinds, load_sems.at[3]))
    loads.append(pltpu.make_async_copy(charges, buffer.at[channel(mine, CHARGE)], load_sems.at[4]))
    loads.append(pltpu.make_async_copy(radii, table, load_sems.at[5]))
    loads.append(pltpu.make_async_copy(tiles, pairs, load_sems.at[6]))
    for load in loads:
        load.start()
    barrier = greet([n[name] for name in PARTNERS])
    clear_unused(buffer)
    pl.semaphore_wait(barrier, len(PARTNERS))

    def ready(c):
        loads[c].wait()
        if c == RADIUS:
            loads[5].wait()
            radius = jnp.zeros((CL, LANES), F32)
            for kind in range(16):
                radius = jnp.where(kinds[...] == kind, table[kind], radius)
            buffer[channel(mine, RADIUS), :] = radius
            loads[6].wait()

    spread(n, buffer, planes, (0, 1, 2, CHARGE, RADIUS), send_sems, recv_sems, ready)


def step_kernel(totals, fixed, velocities, places, planes, moving, partial, landing, send_sems, recv_sems, next_send, next_recv):
    n = neighbours()
    mine = n["mine"]
    barrier = greet([n[name] for name in PARTNERS])
    pl.semaphore_wait(barrier, len(PARTNERS))
    def meanwhile():
        for slot in range(SLOTS):
            for c in (RADIUS, CHARGE):
                places[channel(slot, c), :] = fixed[channel(slot, c), :]
        clear_unused(places)

    force, sent = gather_forces(n, totals, fixed, partial, landing, send_sems, recv_sems, meanwhile)

    def ready(c):
        speed = velocities[c] + time_step * force(c)
        moving[c] = speed
        places[channel(mine, c), :] = fixed[channel(mine, c), :] + time_step * speed

    spread(n, places, planes, range(3), next_send, next_recv, ready)
    for copy in sent:
        copy.wait_send()


def links(k):
    return min(k // 8, 4 - k // 8) + min(k // 2 % 4, 4 - k // 2 % 4) + k % 2


def last_kernel(
    totals, places, moving, destinations, forces_out, arrived, partial, landing, slots, send_sems, recv_sems, out_sems, in_sems, own_sem
):
    z, y, x = here()
    n = neighbours()
    mine = n["mine"]
    others = [(lax.rem(z + k, TOWERS), y, x) for k in range(1, TOWERS)]
    barrier = greet([n["core"], n["cross"]] + others)

    row = jnp.broadcast_to(destinations[...].astype(F32), (CL, CL))
    r = lax.broadcasted_iota(jnp.int32, (CL, CL), 0)
    c = lax.broadcasted_iota(jnp.int32, (CL, CL), 1)
    column = jnp.sum(jnp.where(r == c, row, 0.0), axis=1, keepdims=True)
    rank = jnp.sum(jnp.where((column == row) & (r < c), 1.0, 0.0), axis=0, keepdims=True)
    slot = row[0:1] * CAPACITY + rank
    select = (lax.broadcasted_iota(jnp.int32, (ARRIVING, CL), 0).astype(F32) == slot).astype(BF16)
    select = jnp.concatenate([select] * 3, axis=1)

    pl.semaphore_wait(barrier, 2 + TOWERS - 1)
    def keep(k, value):
        parts = split(value)
        stacked = jnp.concatenate([part.astype(BF16) for part in reversed(parts)], axis=0)
        slots[:, k, :] = jnp.dot(select, stacked, preferred_element_type=F32)

    def meanwhile():
        keep(6, places[channel(mine, CHARGE), :])
        keep(7, places[channel(mine, RADIUS), :])

    force, sent = gather_forces(n, totals, places, partial, landing, send_sems, recv_sems, meanwhile)
    for k in range(3):
        total = force(k)
        forces_out[k] = total
        speed = moving[k] + time_step * total
        keep(3 + k, speed)
        keep(k, places[channel(mine, k), :] + time_step * speed)

    def send(tower):
        return pltpu.make_async_remote_copy(
            slots.at[pl.ds(tower * CAPACITY, CAPACITY)],
            arrived.at[pl.ds(z * CAPACITY, CAPACITY)],
            out_sems.at[tower],
            in_sems.at[z],
            device_id=(tower, y, x),
            device_id_type=MESH,
        )

    def receive(tower):
        return pltpu.make_async_remote_copy(
            slots.at[pl.ds(tower * CAPACITY, CAPACITY)],
            arrived.at[pl.ds(tower * CAPACITY, CAPACITY)],
            out_sems.at[tower],
            in_sems.at[tower],
            device_id=(tower, y, x),
            device_id_type=MESH,
        )

    for k in sorted(range(1, TOWERS), key=links, reverse=True):
        send(lax.rem(z + k, TOWERS)).start()
    own = pltpu.make_async_copy(
        slots.at[pl.ds(z * CAPACITY, CAPACITY)], arrived.at[pl.ds(z * CAPACITY, CAPACITY)], own_sem
    )
    own.start()
    own.wait()
    for k in range(1, TOWERS):
        receive(lax.rem(z + TOWERS - k, TOWERS)).wait_recv()
    for k in range(1, TOWERS):
        send(lax.rem(z + k, TOWERS)).wait_send()
    for copy in sent:
        copy.wait_send()


def params(number):
    return pltpu.CompilerParams(collective_id=number, has_side_effects=True, vmem_limit_bytes=40 * 2**20)


def dma(*counts):
    return pltpu.SemaphoreType.DMA(counts)


def local(positions, velocities, charges, atom_types, type_radius, tiles, tile_live, destinations):
    held = functools.partial(pltpu.with_memory_space_constraint, memory_space=pltpu.HBM)
    shape = functools.partial(jax.ShapeDtypeStruct, dtype=F32)
    blocks = shape((SLOTS * CHANNELS * CL, LANES))
    operands = shape((ROWS * PLANES, LANES))
    partial = pltpu.VMEM((SLOTS, 3, CL, LANES), F32)
    landing = pltpu.VMEM((7, 3, CL, LANES), F32)
    fixed, planes, pairs = pl.pallas_call(
        import_kernel,
        out_shape=(blocks, operands, jax.ShapeDtypeStruct((2, TILES), jnp.int32)),
        in_specs=[HBM] * 5,
        out_specs=(VMEM, VMEM, VMEM),
        scratch_shapes=[pltpu.VMEM((CL, LANES), jnp.int32), pltpu.SMEM((16,), F32), dma(7), dma(5, 5), dma(5, 5)],
        compiler_params=params(0),
    )(*(held(v) for v in (type_radius, jnp.swapaxes(positions, 0, 1), charges, atom_types, tiles.T)))
    totals = tile_forces(pairs, tile_live, planes)
    places, planes, moving = pl.pallas_call(
        step_kernel,
        out_shape=(blocks, operands, shape((3, CL, LANES))),
        in_specs=[VMEM] * 3,
        out_specs=(VMEM, VMEM, VMEM),
        scratch_shapes=[partial, landing, dma(5, 3), dma(5, 3), dma(5, 3), dma(5, 3)],
        compiler_params=params(1),
    )(totals, fixed, jnp.swapaxes(velocities, 0, 1))
    totals = tile_forces(pairs, tile_live, planes)
    forces, arrived = pl.pallas_call(
        last_kernel,
        out_shape=(shape((3, CL, LANES)), shape((ARRIVING, 8, LANES))),
        in_specs=[VMEM] * 4,
        out_specs=(VMEM, VMEM),
        scratch_shapes=[
            partial,
            landing,
            pltpu.VMEM((ARRIVING, 8, LANES), F32),
            dma(5, 3),
            dma(5, 3),
            dma(TOWERS),
            dma(TOWERS),
            pltpu.SemaphoreType.DMA,
        ],
        compiler_params=params(2),
    )(totals, places, moving, destinations.T)
    return jnp.swapaxes(forces, 0, 1), arrived


def solution(mesh):
    home = ("gz", "gy", "gx")
    placed = (
        P(home, None, None),
        P(home, None, None),
        P(home, None),
        P(home, None),
        P(),
        P(home, None),
        P(home),
        P(home, None),
    )
    return jax.shard_map(
        local,
        mesh=mesh,
        in_specs=placed,
        out_specs=(P(home, None, None), P(home, None, None)),
        check_vma=False,
    )
```

```python
import functools

import jax
import jax.numpy as jnp
from jax import lax
from jax.experimental import pallas as pl
from jax.experimental.pallas import tpu as pltpu
from jax.sharding import PartitionSpec as P

coulomb = 0.3
time_step = 0.05

MESH = pl.DeviceIdType.MESH
F32 = jnp.float32
BF16 = jnp.bfloat16

CL = 64
LANES = 128
SLOTS = 6
ROWS = SLOTS * CL
CAPACITY = 4
TILES = 256
TOWERS = 32
ARRIVING = TOWERS * CAPACITY
UNROLL = 32
CENTER = 2.0
PLANES = 32
CHANNELS = 8
RADIUS, CHARGE = 3, 4


def split(x):
    high = x.astype(BF16).astype(F32)
    rest = x - high
    middle = rest.astype(BF16).astype(F32)
    return high, middle, rest - middle


def tile_kernel(listed, live, planes, totals, tiles, list_sem, store_a, store_b):
    listing = pltpu.make_async_copy(listed, tiles, list_sem)
    listing.start()
    line = lax.broadcasted_iota(jnp.int32, (8, LANES), 0)

    def clear(step, carry):
        for k in range(8):
            totals[pl.ds(pl.multiple_of(step * 64, 64) + k * 8, 8), :] = jnp.zeros((8, LANES), F32)
        return carry

    lax.fori_loop(0, ROWS // 8, clear, 0)
    listing.wait()

    sign = jnp.where(line % 4 == 3, 1.0, -1.0).astype(F32)
    live_count = live[0]

    def eight(plane, row):
        return planes[pl.ds(pl.multiple_of(row * 32, 32) + plane * 8, 8), :]

    blank = jnp.zeros((32, LANES), F32)

    def powers_of(group, pair, store):
        lefts, rights = [], []
        for v in range(2):
            a, b = tiles[0, group * UNROLL + 2 * pair + v], tiles[1, group * UNROLL + 2 * pair + v]
            near = eight(0, a) * sign
            lefts += [near, near, eight(1, a) * sign, eight(2, a)]
            r0, r1, r2 = eight(0, b), eight(1, b), eight(2, b)
            rights.append(
                jnp.concatenate([r0, pltpu.roll(r0, 4, 0), pltpu.roll(r1, 4, 0), pltpu.roll(r2, 4, 0)], axis=0)
            )
        left = jnp.concatenate(lefts, axis=0)
        right = jnp.concatenate(
            [jnp.concatenate([rights[0], blank], axis=1), jnp.concatenate([blank, rights[1]], axis=1)], axis=0
        )
        half_dist = lax.dot_general(
            left.astype(BF16), right.astype(BF16), (((0,), (0,)), ((), ())), preferred_element_type=F32
        )
        root = lax.rsqrt(half_dist)
        power = root * root * root
        high = power.astype(BF16)
        store[pair, 0:128, :] = high
        store[pair, 128:256, :] = (power - high.astype(F32)).astype(BF16)

    def sums_of(group, pair, store, sums):
        ids = [(tiles[0, group * UNROLL + 2 * pair + v], tiles[1, group * UNROLL + 2 * pair + v]) for v in range(2)]
        active = [jnp.where(group * UNROLL + 2 * pair + v < live_count, 1.0, 0.0).astype(F32) for v in range(2)]
        from_a = jnp.concatenate([eight(3, ids[v][0]) * active[v] for v in range(2)], axis=0).astype(BF16)
        from_b = jnp.concatenate([eight(3, ids[v][1]) * active[v] for v in range(2)], axis=0).astype(BF16)
        on_right = jnp.dot(jnp.concatenate([from_a, from_a], axis=1), store[pair], preferred_element_type=F32)
        across = jnp.concatenate(
            [
                jnp.concatenate([store[pair, 0:128, 0:128], store[pair, 128:256, 0:128]], axis=1),
                jnp.concatenate([store[pair, 0:128, 128:256], store[pair, 128:256, 128:256]], axis=1),
            ],
            axis=0,
        )
        on_left = lax.dot_general(
            jnp.concatenate([from_b, from_b], axis=1), across, (((1,), (1,)), ((), ())), preferred_element_type=F32
        )
        sums.append((ids[0][0], on_left[0:8, :LANES]))
        sums.append((ids[0][1], on_right[0:8, :LANES]))
        sums.append((ids[1][0], on_left[8:16, LANES:]))
        sums.append((ids[1][1], on_right[8:16, LANES:]))

    def add(sums):
        for row, value in sums:
            at = pl.ds(pl.multiple_of(row * 8, 8), 8)
            totals[at, :] = totals[at, :] + value

    half_group = UNROLL // 2
    for pair in range(half_group):
        powers_of(0, pair, store_a)

    def two_groups(step, carry):
        group = 2 * step
        for now, later, shift in ((store_a, store_b, 1), (store_b, store_a, 2)):
            sums = []
            for pair in range(half_group):
                sums_of(group + shift - 1, pair, now, sums)
                powers_of(jnp.minimum(group + shift, TILES // UNROLL - 1), pair, later)
            add(sums)
        return carry

    lax.fori_loop(0, (live_count + 2 * UNROLL - 1) // (2 * UNROLL), two_groups, 0)


def tile_forces(tiles, live, planes):
    return pl.pallas_call(
        tile_kernel,
        out_shape=jax.ShapeDtypeStruct((ROWS * 8, LANES), F32),
        in_specs=[
            pl.BlockSpec(memory_space=pltpu.VMEM),
            pl.BlockSpec(memory_space=pltpu.SMEM),
            pl.BlockSpec(memory_space=pltpu.VMEM),
        ],
        out_specs=pl.BlockSpec(memory_space=pltpu.VMEM),
        scratch_shapes=[
            pltpu.SMEM((2, TILES), jnp.int32),
            pltpu.SemaphoreType.DMA,
            pltpu.VMEM((UNROLL // 2, 256, 256), BF16),
            pltpu.VMEM((UNROLL // 2, 256, 256), BF16),
        ],
        compiler_params=pltpu.CompilerParams(vmem_limit_bytes=40 * 2**20),
        cost_estimate=pl.CostEstimate(flops=256 * 128 * 128 * 120, bytes_accessed=2 * 2**20, transcendentals=256 * 128 * 128),
    )(tiles, live, planes)


VMEM = pl.BlockSpec(memory_space=pltpu.VMEM)
HBM = pl.BlockSpec(memory_space=pltpu.HBM)
SMEM = pl.BlockSpec(memory_space=pltpu.SMEM)
BELOW, ABOVE = 4, 5


def here():
    return lax.axis_index("gz"), lax.axis_index("gy"), lax.axis_index("gx")


def neighbours():
    z, y, x = here()
    even = lax.rem(z, 2) == 0
    step = 1 - 2 * lax.rem(z, 2)
    pair = z + step
    return dict(
        core=(z, 1 - y, x),
        pair=(pair, y, x),
        cross=(pair, y, 1 - x),
        ahead=(lax.rem(z + 2 * step + TOWERS, TOWERS), y, x),
        behind=(lax.rem(z - 2 * step + TOWERS, TOWERS), y, x),
        mine=y * 2 + x,
        core_slot=(1 - y) * 2 + x,
        plate_slot=y * 2 + 1 - x,
        far_slot=(1 - y) * 2 + 1 - x,
        pair_slot=ABOVE - lax.rem(z, 2),
        other_slot=BELOW + lax.rem(z, 2),
    )


PARTNERS = ("core", "pair", "cross", "ahead", "behind")


def greet(devices):
    barrier = pltpu.get_barrier_semaphore()
    for device in devices:
        pl.semaphore_signal(barrier, inc=1, device_id=device, device_id_type=MESH)
    return barrier


def channel(slot, c):
    return pl.ds(pl.multiple_of(slot * (CHANNELS * CL) + c * CL, CL), CL)


def prepare(slot, blocks, planes):
    line = lax.broadcasted_iota(jnp.int32, (8, LANES), 0)
    upper = line < 4
    center = jnp.where(line < 3, CENTER, 0.0).astype(F32)

    def eight_clusters(step, carry):
        for k in range(8):
            first = pl.multiple_of(slot * (CHANNELS * CL) + step * 8, 8) + k
            to = pl.multiple_of(slot * (CL * PLANES) + step * (8 * PLANES), 8 * PLANES) + k * PLANES
            loaded = blocks[pl.ds(first, 8, stride=CL), :] - center
            twice = jnp.where(upper, loaded, pltpu.roll(loaded, 4, 0))
            charge = jnp.broadcast_to(loaded[4:5, :], (8, LANES))
            high, middle, low = split(twice)
            planes[pl.ds(to, 8), :] = jnp.where(upper, high, middle)
            planes[pl.ds(to + 8, 8), :] = jnp.where(upper, low, high)
            square = twice * twice
            square = square + pltpu.roll(square, 2, 0)
            square = 0.5 * (square + pltpu.roll(square, 1, 0))
            high, middle, low = split(square)
            parts = jnp.where(line == 0, high, jnp.where(line == 1, middle, low))
            planes[pl.ds(to + 16, 8), :] = jnp.where(line < 3, parts, jnp.where((line == 3) | (line == 7), 0.0, 1.0))
            weighted = jnp.where((line == 3) | (line == 7), 1.0, twice) * charge
            high = weighted.astype(BF16).astype(F32)
            planes[pl.ds(to + 24, 8), :] = jnp.where(upper, high, weighted - high)
        return carry

    lax.fori_loop(0, CL // 8, eight_clusters, 0)


def finish(slot, totals, blocks, partial):
    factor = coulomb * 0.5**1.5

    def eight_clusters(step, carry):
        rows = pl.ds(pl.multiple_of(step * 8, 8), 8)

        def plane(c):
            return blocks[pl.ds(pl.multiple_of(slot * (CHANNELS * CL) + c * CL + step * 8, 8), 8), :]

        def summed(k):
            first = pl.multiple_of(slot * (CL * 8) + step * 64, 64) + k
            return totals[pl.ds(first, 8, stride=8), :] + totals[pl.ds(first + 4, 8, stride=8), :]

        scale = factor * plane(CHARGE)
        whole = summed(3)
        for c in range(3):
            partial[slot, c, rows, :] = scale * ((plane(c) - CENTER) * whole - summed(c))
        return carry

    lax.fori_loop(0, CL // 8, eight_clusters, 0)


def clear_unused(blocks):
    for slot in range(SLOTS):
        for c in range(5, CHANNELS):
            blocks[channel(slot, c), :] = jnp.zeros((CL, LANES), F32)


def remote(source, target, send_sems, recv_sems, way, chunk, device):
    return pltpu.make_async_remote_copy(
        source, target, send_sems.at[way, chunk], recv_sems.at[way, chunk], device_id=device, device_id_type=MESH
    )


def spread(n, buffer, planes, channels, send_sems, recv_sems, ready):
    sent = []

    def send(way, chunk, slot, there, name):
        copy = remote(buffer.at[channel(slot, chunk)], buffer.at[channel(there, chunk)], send_sems, recv_sems, way, chunk, n[name])
        copy.start()
        sent.append(copy)

    def arrive(way, chunk, slot):
        place = buffer.at[channel(slot, chunk)]
        remote(place, place, send_sems, recv_sems, way, chunk, n["core"]).wait_recv()

    for c in channels:
        ready(c)
        send(1, c, n["mine"], n["other_slot"], "pair")
        send(0, c, n["mine"], n["mine"], "core")
    prepare(n["mine"], buffer, planes)
    for c in channels:
        arrive(1, c, n["pair_slot"])
        send(2, c, n["pair_slot"], n["mine"], "cross")
        send(3, c, n["pair_slot"], n["other_slot"], "ahead")
    prepare(n["pair_slot"], buffer, planes)
    for c in channels:
        arrive(0, c, n["core_slot"])
    prepare(n["core_slot"], buffer, planes)
    for c in channels:
        arrive(2, c, n["plate_slot"])
        send(4, c, n["plate_slot"], n["plate_slot"], "core")
    prepare(n["plate_slot"], buffer, planes)
    for c in channels:
        arrive(4, c, n["far_slot"])
    prepare(n["far_slot"], buffer, planes)
    for c in channels:
        arrive(3, c, n["other_slot"])
    prepare(n["other_slot"], buffer, planes)
    for copy in sent:
        copy.wait_send()


def gather_forces(n, totals, blocks, partial, landing, send_sems, recv_sems, meanwhile):
    sent = []

    def send(way, chunk, source, name):
        copy = remote(source, landing.at[way, chunk], send_sems, recv_sems, way, chunk, n[name])
        copy.start()
        sent.append(copy)

    def arrive(way, chunk):
        place = landing.at[way, chunk]
        remote(place, place, send_sems, recv_sems, way, chunk, n["core"]).wait_recv()

    for way, slot, name in ((2, "other_slot", "behind"), (0, "far_slot", "core"), (4, "core_slot", "core")):
        finish(n[slot], totals, blocks, partial)
        for c in range(3):
            send(way, c, partial.at[n[slot], c], name)
    for slot in ("plate_slot", "pair_slot", "mine"):
        finish(n[slot], totals, blocks, partial)
    meanwhile()
    for c in range(3):
        arrive(0, c)
        landing[5, c] = partial[n["plate_slot"], c] + landing[0, c]
        send(1, c, landing.at[5, c], "cross")
    for c in range(3):
        arrive(1, c)
        arrive(2, c)
        landing[6, c] = partial[n["pair_slot"], c] + landing[1, c] + landing[2, c]
        send(3, c, landing.at[6, c], "pair")

    def total(c):
        arrive(3, c)
        arrive(4, c)
        return partial[n["mine"], c] + landing[3, c] + landing[4, c]

    return total, sent


def import_kernel(radii, positions, charges, types, tiles, buffer, planes, pairs, kinds, table, load_sems, send_sems, recv_sems):
    n = neighbours()
    mine = n["mine"]
    loads = [pltpu.make_async_copy(positions.at[c], buffer.at[channel(mine, c)], load_sems.at[c]) for c in range(3)]
    loads.append(pltpu.make_async_copy(types, kinds, load_sems.at[3]))
    loads.append(pltpu.make_async_copy(charges, buffer.at[channel(mine, CHARGE)], load_sems.at[4]))
    loads.append(pltpu.make_async_copy(radii, table, load_sems.at[5]))
    loads.append(pltpu.make_async_copy(tiles, pairs, load_sems.at[6]))
    for load in loads:
        load.start()
    barrier = greet([n[name] for name in PARTNERS])
    clear_unused(buffer)
    pl.semaphore_wait(barrier, len(PARTNERS))

    def ready(c):
        loads[c].wait()
        if c == RADIUS:
            loads[5].wait()
            radius = jnp.zeros((CL, LANES), F32)
            for kind in range(16):
                radius = jnp.where(kinds[...] == kind, table[kind], radius)
            buffer[channel(mine, RADIUS), :] = radius
            loads[6].wait()

    spread(n, buffer, planes, (0, 1, 2, CHARGE, RADIUS), send_sems, recv_sems, ready)


def step_kernel(totals, fixed, velocities, places, planes, moving, partial, landing, send_sems, recv_sems, next_send, next_recv):
    n = neighbours()
    mine = n["mine"]
    barrier = greet([n[name] for name in PARTNERS])
    pl.semaphore_wait(barrier, len(PARTNERS))
    def meanwhile():
        for slot in range(SLOTS):
            for c in (RADIUS, CHARGE):
                places[channel(slot, c), :] = fixed[channel(slot, c), :]
        clear_unused(places)

    force, sent = gather_forces(n, totals, fixed, partial, landing, send_sems, recv_sems, meanwhile)

    def ready(c):
        speed = velocities[c] + time_step * force(c)
        moving[c] = speed
        places[channel(mine, c), :] = fixed[channel(mine, c), :] + time_step * speed

    spread(n, places, planes, range(3), next_send, next_recv, ready)
    for copy in sent:
        copy.wait_send()


def links(k):
    return min(k // 8, 4 - k // 8) + min(k // 2 % 4, 4 - k // 2 % 4) + k % 2


def last_kernel(
    totals, places, moving, destinations, forces_out, arrived, partial, landing, slots, send_sems, recv_sems, out_sems, in_sems, own_sem
):
    z, y, x = here()
    n = neighbours()
    mine = n["mine"]
    others = [(lax.rem(z + k, TOWERS), y, x) for k in range(1, TOWERS)]
    barrier = greet([n["core"], n["cross"]] + others)

    row = jnp.broadcast_to(destinations[...].astype(F32), (CL, CL))
    r = lax.broadcasted_iota(jnp.int32, (CL, CL), 0)
    c = lax.broadcasted_iota(jnp.int32, (CL, CL), 1)
    column = jnp.sum(jnp.where(r == c, row, 0.0), axis=1, keepdims=True)
    rank = jnp.sum(jnp.where((column == row) & (r < c), 1.0, 0.0), axis=0, keepdims=True)
    slot = row[0:1] * CAPACITY + rank
    select = (lax.broadcasted_iota(jnp.int32, (ARRIVING, CL), 0).astype(F32) == slot).astype(BF16)
    select = jnp.concatenate([select] * 3, axis=1)

    pl.semaphore_wait(barrier, 2 + TOWERS - 1)
    def keep(first, value, second, other):
        parts = split(jnp.concatenate([value, other], axis=1))
        stacked = jnp.concatenate([part.astype(BF16) for part in reversed(parts)], axis=0)
        chosen = jnp.dot(select, stacked, preferred_element_type=F32)
        slots[:, first, :] = chosen[:, :LANES]
        slots[:, second, :] = chosen[:, LANES:]

    def meanwhile():
        keep(6, places[channel(mine, CHARGE), :], 7, places[channel(mine, RADIUS), :])

    force, sent = gather_forces(n, totals, places, partial, landing, send_sems, recv_sems, meanwhile)
    for k in range(3):
        total = force(k)
        forces_out[k] = total
        speed = moving[k] + time_step * total
        keep(3 + k, speed, k, places[channel(mine, k), :] + time_step * speed)

    def send(tower):
        return pltpu.make_async_remote_copy(
            slots.at[pl.ds(tower * CAPACITY, CAPACITY)],
            arrived.at[pl.ds(z * CAPACITY, CAPACITY)],
            out_sems.at[tower],
            in_sems.at[z],
            device_id=(tower, y, x),
            device_id_type=MESH,
        )

    def receive(tower):
        return pltpu.make_async_remote_copy(
            slots.at[pl.ds(tower * CAPACITY, CAPACITY)],
            arrived.at[pl.ds(tower * CAPACITY, CAPACITY)],
            out_sems.at[tower],
            in_sems.at[tower],
            device_id=(tower, y, x),
            device_id_type=MESH,
        )

    for k in sorted(range(1, TOWERS), key=links, reverse=True):
        send(lax.rem(z + k, TOWERS)).start()
    own = pltpu.make_async_copy(
        slots.at[pl.ds(z * CAPACITY, CAPACITY)], arrived.at[pl.ds(z * CAPACITY, CAPACITY)], own_sem
    )
    own.start()
    own.wait()
    for k in range(1, TOWERS):
        receive(lax.rem(z + TOWERS - k, TOWERS)).wait_recv()
    for k in range(1, TOWERS):
        send(lax.rem(z + k, TOWERS)).wait_send()
    for copy in sent:
        copy.wait_send()


def params(number):
    return pltpu.CompilerParams(collective_id=number, has_side_effects=True, vmem_limit_bytes=40 * 2**20)


def dma(*counts):
    return pltpu.SemaphoreType.DMA(counts)


def local(positions, velocities, charges, atom_types, type_radius, tiles, tile_live, destinations):
    held = functools.partial(pltpu.with_memory_space_constraint, memory_space=pltpu.HBM)
    shape = functools.partial(jax.ShapeDtypeStruct, dtype=F32)
    blocks = shape((SLOTS * CHANNELS * CL, LANES))
    operands = shape((ROWS * PLANES, LANES))
    partial = pltpu.VMEM((SLOTS, 3, CL, LANES), F32)
    landing = pltpu.VMEM((7, 3, CL, LANES), F32)
    fixed, planes, pairs = pl.pallas_call(
        import_kernel,
        out_shape=(blocks, operands, jax.ShapeDtypeStruct((2, TILES), jnp.int32)),
        in_specs=[HBM] * 5,
        out_specs=(VMEM, VMEM, VMEM),
        scratch_shapes=[pltpu.VMEM((CL, LANES), jnp.int32), pltpu.SMEM((16,), F32), dma(7), dma(5, 5), dma(5, 5)],
        compiler_params=params(0),
    )(*(held(v) for v in (type_radius, jnp.swapaxes(positions, 0, 1), charges, atom_types, tiles.T)))
    totals = tile_forces(pairs, tile_live, planes)
    places, planes, moving = pl.pallas_call(
        step_kernel,
        out_shape=(blocks, operands, shape((3, CL, LANES))),
        in_specs=[VMEM] * 3,
        out_specs=(VMEM, VMEM, VMEM),
        scratch_shapes=[partial, landing, dma(5, 3), dma(5, 3), dma(5, 3), dma(5, 3)],
        compiler_params=params(1),
    )(totals, fixed, jnp.swapaxes(velocities, 0, 1))
    totals = tile_forces(pairs, tile_live, planes)
    forces, arrived = pl.pallas_call(
        last_kernel,
        out_shape=(shape((3, CL, LANES)), shape((ARRIVING, 8, LANES))),
        in_specs=[VMEM] * 4,
        out_specs=(VMEM, VMEM),
        scratch_shapes=[
            partial,
            landing,
            pltpu.VMEM((ARRIVING, 8, LANES), F32),
            dma(5, 3),
            dma(5, 3),
            dma(TOWERS),
            dma(TOWERS),
            pltpu.SemaphoreType.DMA,
        ],
        compiler_params=params(2),
    )(totals, places, moving, destinations.T)
    return jnp.swapaxes(forces, 0, 1), arrived


def solution(mesh):
    home = ("gz", "gy", "gx")
    placed = (
        P(home, None, None),
        P(home, None, None),
        P(home, None),
        P(home, None),
        P(),
        P(home, None),
        P(home),
        P(home, None),
    )
    return jax.shard_map(
        local,
        mesh=mesh,
        in_specs=placed,
        out_specs=(P(home, None, None), P(home, None, None)),
        check_vma=False,
    )
```
